512 devices in a mesh: rows: 16 (over z, core), feats: 32 (over x, y).
Axes of the slice: x: 4, y: 8, z: 8, core: 2. Of those that a mesh axis runs over, the one named last changes fastest.
Arguments:
- bin_index: int32 [2048, 32768], P('feats', 'rows'), may hold values from 0 to 255
- gradient: bfloat16 [32768], P('rows'), may hold values from -6 to 6
- hessian: bfloat16 [32768], P('rows'), may hold values from 0.049804688 to 1
- node_id: int32 [32768], P('rows'), may hold values from 0 to 15
- split_feature: int32 [16], replicated, may hold values from 0 to 2047
- split_bin: int32 [16], replicated, may hold values from 0 to 255
Outputs:
- split_gain: float32 [2048, 16, 256], P(('feats', 'rows'))
- best_gain: float32 [16], replicated
- child_id: int32 [32768], P('rows')
The draws below stay inside these ranges and needn't reach their ends.
All inputs are finite; a program needn't handle non-finite values.
Results may differ from the reference program's by a relative error of at most 0.0003.
Values may be sent and summed in bfloat16 or wider, within the bound.
A program may use at most 64 MiB of HBM per device.

```python
import math
import jax
import jax.numpy as jnp
from jax import lax

FEATURES = 2048
BINS = 256
NODES = 16
ROWS_ALL = 32768


def plant(entries, stream_key, least, high):
    spot = [jax.random.randint(jax.random.fold_in(stream_key, axis), (), 0, length) for axis, length in enumerate(entries.shape)]
    main_axis = entries.shape.index(max(entries.shape))
    neighbour = spot[:main_axis] + [(spot[main_axis] + 1) % entries.shape[main_axis]] + spot[main_axis + 1:]
    return entries.at[tuple(spot)].set(least).at[tuple(neighbour)].set(high)


def level_of(rng, extent, shards, least, top_value):
    def one(dim, blocks):
        heights = jax.random.uniform(jax.random.fold_in(jax.random.fold_in(rng, 6), dim), (blocks,), jnp.float32, least / len(shards), top_value / len(shards))
        return jnp.repeat(jnp.exp(heights), extent[dim] // blocks).reshape((-1,) + (1,) * (len(extent) - dim - 1))

    level = one(*shards[0])
    for cut in shards[1:]:
        level = level * one(*cut)
    return level


def noise(own_key, extent, spread, limit, pieces=(), kind=jnp.bfloat16):
    drawn = jax.random.normal(own_key, extent, jnp.float32) * spread
    if len(pieces) > 0:
        drawn = level_of(own_key, extent, pieces, -0.22, 0.18) * drawn
    return jnp.clip(drawn, min=-limit, max=limit).astype(kind)


def setup_inputs(seed: int = 0) -> dict:
    streams_of = jax.random.split(jax.random.key(seed), 7)
    return {
        "bin_index": plant(jax.random.randint(streams_of[0], (FEATURES, ROWS_ALL), 0, BINS), jax.random.fold_in(streams_of[0], 1), 0, BINS - 1).astype(jnp.int32),
        "gradient": noise(streams_of[1], (ROWS_ALL,), 1.0, 6.0, ((0, 16),)),
        "hessian": jnp.clip(jnp.exp(math.log(1.0) - 2.9996462 * jax.random.uniform(streams_of[2], (ROWS_ALL,), jnp.float32) ** level_of(streams_of[2], (ROWS_ALL,), ((0, 16),), -0.2, 0.2)), 0.049804688, 1.0).astype(jnp.bfloat16),
        "node_id": plant(jax.random.randint(streams_of[3], (ROWS_ALL,), 0, NODES), jax.random.fold_in(streams_of[3], 1), 0, NODES - 1).astype(jnp.int32),
        "split_feature": plant(jax.random.randint(streams_of[4], (NODES,), 0, FEATURES), jax.random.fold_in(streams_of[4], 1), 0, FEATURES - 1).astype(jnp.int32),
        "split_bin": plant(jax.random.randint(streams_of[5], (NODES,), 0, BINS), jax.random.fold_in(streams_of[5], 1), 0, BINS - 1).astype(jnp.int32),
    }


def reference(bin_index, gradient, hessian, node_id, split_feature, split_bin):
    weights = jnp.stack([gradient.astype(jnp.float32), hessian.astype(jnp.float32)], axis=1)

    def per_feature(column):
        segment = node_id * BINS + column
        summed = jax.ops.segment_sum(weights, segment, num_segments=NODES * BINS)
        return summed.T.reshape(2, NODES, BINS)

    hist = lax.map(per_feature, bin_index)
    grad_hist = hist[:, 0]
    hess_hist = hist[:, 1]
    left_grad = jnp.cumsum(grad_hist, axis=2)
    left_hess = jnp.cumsum(hess_hist, axis=2)
    total_grad = left_grad[:, :, -1:]
    total_hess = left_hess[:, :, -1:]
    split_gain = (left_grad * left_grad / (left_hess + 1.0)
                  + (total_grad - left_grad) ** 2 / (total_hess - left_hess + 1.0)
                  - total_grad * total_grad / (total_hess + 1.0))
    best_gain = jnp.max(split_gain, axis=(0, 2))
    feature_of_row = split_feature[node_id]
    chosen = jnp.take_along_axis(bin_index, feature_of_row[None, :], axis=0)[0]
    right = (chosen > split_bin[node_id]).astype(jnp.int32)
    child_id = 2 * node_id + right
    return split_gain, best_gain, child_id
```

```python
import functools

import jax
import jax.numpy as jnp
from jax import lax
from jax.experimental import pallas as pl
from jax.experimental.pallas import tpu as pltpu
from jax.sharding import PartitionSpec as P

BINS = 256
LO = 64
HI = BINS // LO
NODES = 16
LANES = 128
BF16 = jnp.bfloat16
MESH = pl.DeviceIdType.MESH


def sublane_index(rows, lanes):
    return lax.broadcasted_iota(jnp.int32, (rows, lanes), 0)


def as_bf16(x):
    return x.astype(jnp.float32).astype(BF16)


def kernel(R, F, own, sf_ref, sb_ref, bins_ref, grad_ref, hess_ref, node_ref, node_row_ref,
           gain_ref, best_ref, child_ref,
           bins_v, picked, send, recv, acc, right, rights, top, tops, high, highs,
           in_sem, send_sem, recv_sem, rsend_sem, rrecv_sem, tsend_sem, trecv_sem, hsend_sem, hrecv_sem):
    feat_local, row_count = bins_v.shape
    tiles = row_count // LANES
    me_r = lax.axis_index("rows")
    me_f = lax.axis_index("feats")

    load = pltpu.make_async_copy(bins_ref, bins_v, in_sem)
    load.start()

    barrier = pltpu.get_barrier_semaphore()

    def greet_rows(k, c):
        pl.semaphore_signal(barrier, inc=1, device_id=(lax.rem(me_r + k, R), me_f), device_id_type=MESH)
        return c

    def greet_feats(k, c):
        pl.semaphore_signal(barrier, inc=1, device_id=(me_r, lax.rem(me_f + k, F)), device_id_type=MESH)
        return c

    lax.fori_loop(1, R, greet_rows, 0)
    lax.fori_loop(1, F, greet_feats, 0)

    grad = grad_ref[...]
    hess = hess_ref[...]
    node = node_ref[...]
    node16 = as_bf16(node)
    load.wait()
    for j in range(R):
        block = bins_v[j * own:(j + 1) * own, :]
        stacked = jnp.concatenate([block[:, t * LANES:(t + 1) * LANES] for t in range(tiles)], axis=0)
        send[j, 0:own * tiles, :] = as_bf16(stacked)
        send[j, own * tiles:(own + 1) * tiles, :] = grad
        send[j, (own + 1) * tiles:(own + 2) * tiles, :] = hess
        send[j, (own + 2) * tiles:(own + 3) * tiles, :] = node16
    recv[0] = send[me_r]

    pl.semaphore_wait(barrier, R + F - 2)

    def offset(i):
        odd = lax.rem(i, 2)
        return odd * ((i + 1) // 2) + (1 - odd) * lax.rem(R - i // 2, R)

    def chunk_copy(k):
        to = lax.rem(me_r + k, R)
        return pltpu.make_async_remote_copy(
            src_ref=send.at[to], dst_ref=recv.at[k], send_sem=send_sem.at[k], recv_sem=recv_sem.at[k],
            device_id=(to, me_f), device_id_type=MESH)

    def right_copy(k):
        return pltpu.make_async_remote_copy(
            src_ref=right, dst_ref=rights.at[k], send_sem=rsend_sem.at[k], recv_sem=rrecv_sem.at[k],
            device_id=(me_r, lax.rem(me_f + k, F)), device_id_type=MESH)

    def top_copy(k):
        return pltpu.make_async_remote_copy(
            src_ref=top, dst_ref=tops.at[k], send_sem=tsend_sem.at[k], recv_sem=trecv_sem.at[k],
            device_id=(lax.rem(me_r + k, R), me_f), device_id_type=MESH)

    def high_copy(k):
        return pltpu.make_async_remote_copy(
            src_ref=high, dst_ref=highs.at[k], send_sem=hsend_sem.at[k], recv_sem=hrecv_sem.at[k],
            device_id=(me_r, lax.rem(me_f + k, F)), device_id_type=MESH)

    def start(copy, k, c):
        copy(k).start()
        return c

    def wait_recv(copy, k, c):
        copy(k).wait_recv()
        return c

    def wait_send(copy, k, c):
        copy(k).wait_send()
        return c

    lax.fori_loop(1, R, lambda i, c: start(chunk_copy, offset(i), c), 0)

    first = me_f * feat_local
    split = jnp.zeros((NODES, LANES), jnp.int32)
    mine = jnp.zeros((NODES, LANES), jnp.int32)
    index = sublane_index(NODES, LANES)
    for n in range(NODES):
        column = sf_ref[n] - first
        held = jnp.where(column >= 0, 1, 0) * jnp.where(column < feat_local, 1, 0)
        picked[n:n + 1, :] = bins_v[pl.ds(jnp.clip(column, 0, feat_local - 1), 1), :]
        split = jnp.where(index == n, sb_ref[n], split)
        mine = jnp.where(index == n, held, mine)
    node_row = node_row_ref[...]
    parts = []
    for t in range(tiles):
        lanes = slice(t * LANES, (t + 1) * LANES)
        goes = jnp.where(picked[:, lanes] > split, mine, 0)
        goes = jnp.where(jnp.broadcast_to(node_row[:, lanes], (NODES, LANES)) == index, goes, 0)
        parts.append(jnp.sum(goes.astype(jnp.float32), axis=0, keepdims=True))
    right[...] = jnp.concatenate(parts, axis=0).astype(BF16)
    lax.fori_loop(1, F, lambda k, c: start(right_copy, k, c), 0)

    acc[...] = jnp.zeros_like(acc)
    span = 4
    depth = span * LANES
    zero = jnp.zeros((NODES, depth), BF16)

    def over_lanes(slot, base, q, stride, rows):
        return jnp.concatenate(
            [jnp.broadcast_to(recv[slot, pl.ds(base + (q * span + s) * stride, 1), :], (rows, LANES))
             for s in range(span)], axis=1)

    def add_chunk(slot):
        for q in range(tiles // span):
            here = over_lanes(slot, (own + 2) * tiles, q, 1, NODES) == as_bf16(sublane_index(NODES, depth))
            wg = jnp.where(here, over_lanes(slot, own * tiles, q, 1, NODES), zero)
            wh = jnp.where(here, over_lanes(slot, (own + 1) * tiles, q, 1, NODES), zero)
            levels = as_bf16(sublane_index(LO, depth))
            for f in range(own):
                b = over_lanes(slot, f, q, own, 1).astype(jnp.float32)
                hi = jnp.floor(b * (1.0 / LO))
                lo = (b - hi * LO).astype(BF16)
                hi = jnp.broadcast_to(hi.astype(BF16), (NODES, depth))
                sides = []
                for level in range(HI):
                    at = hi == BF16(level)
                    sides += [jnp.where(at, wg, zero), jnp.where(at, wh, zero)]
                moving = jnp.concatenate(sides, axis=0)
                steps = jnp.where(jnp.broadcast_to(lo, (LO, depth)) <= levels, BF16(1), BF16(0))
                acc[f] += lax.dot_general(
                    moving, steps, (((1,), (1,)), ((), ())), preferred_element_type=jnp.float32)

    add_chunk(0)

    def one_source(i, c):
        k = offset(i)
        chunk_copy(k).wait_recv()
        add_chunk(k)
        return c

    lax.fori_loop(1, R, one_source, 0)

    best = jnp.full((NODES, 1), -jnp.inf, jnp.float32)
    for f in range(own):
        blocks = []
        carry = jnp.zeros((2 * NODES, 1), jnp.float32)
        for level in range(HI):
            block = acc[f, level * 2 * NODES:(level + 1) * 2 * NODES, :] + carry
            carry = block[:, LO - 1:LO]
            blocks.append(block)
        left = jnp.concatenate(blocks, axis=1)
        left_grad, left_hess = left[:NODES], left[NODES:]
        total_grad, total_hess = carry[:NODES], carry[NODES:]
        right_grad = total_grad - left_grad
        gain = (left_grad * left_grad / (left_hess + 1.0)
                + right_grad * right_grad / (total_hess - left_hess + 1.0)
                - total_grad * total_grad / (total_hess + 1.0))
        gain_ref[f] = gain
        best = jnp.maximum(best, jnp.max(gain, axis=1, keepdims=True))

    diagonal = index == lax.broadcasted_iota(jnp.int32, (NODES, LANES), 1)
    top[...] = jnp.max(jnp.where(diagonal, best, -jnp.inf), axis=0, keepdims=True)
    tops[0] = top[...]
    lax.fori_loop(1, R, lambda k, c: start(top_copy, k, c), 0)

    rights[0] = right[...]
    lax.fori_loop(1, F, lambda k, c: wait_recv(right_copy, k, c), 0)
    goes_right = jnp.zeros((tiles, LANES), jnp.float32)
    for k in range(F):
        goes_right = goes_right + rights[k].astype(jnp.float32)
    child_ref[...] = 2 * node + goes_right.astype(jnp.int32)

    lax.fori_loop(1, R, lambda k, c: wait_recv(top_copy, k, c), 0)
    high[...] = jnp.max(tops[...], axis=0)
    highs[0] = high[...]
    lax.fori_loop(1, F, lambda k, c: start(high_copy, k, c), 0)
    lax.fori_loop(1, R, lambda k, c: wait_send(chunk_copy, k, c), 0)
    lax.fori_loop(1, F, lambda k, c: wait_send(right_copy, k, c), 0)
    lax.fori_loop(1, R, lambda k, c: wait_send(top_copy, k, c), 0)
    lax.fori_loop(1, F, lambda k, c: wait_recv(high_copy, k, c), 0)
    best_ref[...] = jnp.max(highs[...], axis=0)
    lax.fori_loop(1, F, lambda k, c: wait_send(high_copy, k, c), 0)


def on_device(R, F, bin_index, gradient, hessian, node_id, split_feature, split_bin):
    feat_local, row_count = bin_index.shape
    own = feat_local // R
    tiles = row_count // LANES
    rows = (own + 3) * tiles
    vmem = pl.BlockSpec(memory_space=pltpu.VMEM)
    smem = pl.BlockSpec(memory_space=pltpu.SMEM)
    dma = pltpu.SemaphoreType.DMA
    gain, best, child = pl.pallas_call(
        functools.partial(kernel, R, F, own),
        out_shape=(
            jax.ShapeDtypeStruct((own, NODES, BINS), jnp.float32),
            jax.ShapeDtypeStruct((1, LANES), jnp.float32),
            jax.ShapeDtypeStruct((tiles, LANES), jnp.int32),
        ),
        in_specs=[smem, smem, pl.BlockSpec(memory_space=pl.ANY), vmem, vmem, vmem, vmem],
        out_specs=(vmem, vmem, vmem),
        scratch_shapes=[
            pltpu.VMEM((feat_local, row_count), jnp.int32),
            pltpu.VMEM((NODES, row_count), jnp.int32),
            pltpu.VMEM((R, rows, LANES), BF16),
            pltpu.VMEM((R, rows, LANES), BF16),
            pltpu.VMEM((own, 2 * NODES * HI, LO), jnp.float32),
            pltpu.VMEM((tiles, LANES), BF16),
            pltpu.VMEM((F, tiles, LANES), BF16),
            pltpu.VMEM((1, LANES), jnp.float32),
            pltpu.VMEM((R, 1, LANES), jnp.float32),
            pltpu.VMEM((1, LANES), jnp.float32),
            pltpu.VMEM((F, 1, LANES), jnp.float32),
            dma(()),
            dma((R,)), dma((R,)),
            dma((F,)), dma((F,)),
            dma((R,)), dma((R,)),
            dma((F,)), dma((F,)),
        ],
        compiler_params=pltpu.CompilerParams(
            collective_id=0, has_side_effects=True, vmem_limit_bytes=32 << 20),
    )(
        split_feature, split_bin, bin_index,
        gradient.reshape(tiles, LANES), hessian.reshape(tiles, LANES),
        node_id.reshape(tiles, LANES), node_id.reshape(1, row_count),
    )
    return gain, best[0, :NODES], child.reshape(row_count)


def solution(mesh):
    return jax.shard_map(
        functools.partial(on_device, mesh.shape["rows"], mesh.shape["feats"]),
        mesh=mesh,
        in_specs=(P("feats", "rows"), P("rows"), P("rows"), P("rows"), P(), P()),
        out_specs=(P(("feats", "rows"), None, None), P(), P("rows")),
        check_vma=False,
    )
```

```python
import functools

import jax
import jax.numpy as jnp
from jax import lax
from jax.experimental import pallas as pl
from jax.experimental.pallas import tpu as pltpu
from jax.sharding import PartitionSpec as P

BINS = 256
LO = 64
HI = BINS // LO
NODES = 16
LANES = 128
BF16 = jnp.bfloat16
MESH = pl.DeviceIdType.MESH
FIRST = 3


def sublane_index(rows, lanes):
    return lax.broadcasted_iota(jnp.int32, (rows, lanes), 0)


def as_bf16(x):
    return x.astype(jnp.float32).astype(BF16)


def kernel(R, F, own, sf_ref, sb_ref, bins_ref, grad_ref, hess_ref, node_ref, node_row_ref,
           gain_ref, best_ref, child_ref,
           bins_v, picked, node_v, node_row_v, send, recv, weights, acc, right, rights, top, tops, high, highs,
           in_sem, send_sem, recv_sem, wsend_sem, wrecv_sem, fsend_sem, frecv_sem,
           rsend_sem, rrecv_sem, tsend_sem, trecv_sem, hsend_sem, hrecv_sem):
    feat_local, row_count = bins_v.shape
    tiles = row_count // LANES
    Z = R // 2
    me_r = lax.axis_index("rows")
    me_f = lax.axis_index("feats")
    me_z = me_r // 2
    core = lax.rem(me_r, 2)

    loads = [
        pltpu.make_async_copy(bins_ref, bins_v, in_sem.at[0]),
        pltpu.make_async_copy(grad_ref, weights.at[0, 0, 0:tiles, :], in_sem.at[1]),
        pltpu.make_async_copy(hess_ref, weights.at[0, 0, tiles:2 * tiles, :], in_sem.at[2]),
        pltpu.make_async_copy(node_ref, node_v, in_sem.at[3]),
        pltpu.make_async_copy(node_row_ref, node_row_v, in_sem.at[4]),
    ]
    for load in loads:
        load.start()

    barrier = pltpu.get_barrier_semaphore()

    def greet_rows(k, c):
        pl.semaphore_signal(barrier, inc=1, device_id=(lax.rem(me_r + k, R), me_f), device_id_type=MESH)
        return c

    def greet_feats(k, c):
        pl.semaphore_signal(barrier, inc=1, device_id=(me_r, lax.rem(me_f + k, F)), device_id_type=MESH)
        return c

    lax.fori_loop(F // 2, F, greet_feats, 0)
    lax.fori_loop(1, F // 2, greet_feats, 0)
    lax.fori_loop(1, R, greet_rows, 0)

    for load in loads:
        load.wait()
    weights[0, 0, 2 * tiles:3 * tiles, :] = as_bf16(node_v[...])
    for j in range(R):
        block = bins_v[j * own:(j + 1) * own, :]
        send[j] = as_bf16(jnp.concatenate([block[:, t * LANES:(t + 1) * LANES] for t in range(tiles)], axis=0))
    recv[0, 0] = send[me_r]

    pl.semaphore_wait(barrier, R + F - 2)

    def bins_copy(d, o):
        to = 2 * lax.rem(me_z + d, Z) + (core if o == 0 else 1 - core)
        return bins_copy_to(d, o, to)

    def bins_copy_from(d, o):
        return bins_copy_to(d, o, 2 * me_z + 1 - core)

    def bins_copy_to(d, o, to):
        return pltpu.make_async_remote_copy(
            src_ref=send.at[to], dst_ref=recv.at[d, o], send_sem=send_sem.at[d, o], recv_sem=recv_sem.at[d, o],
            device_id=(to, me_f), device_id_type=MESH)

    def weights_copy(d):
        return pltpu.make_async_remote_copy(
            src_ref=weights.at[0, 0], dst_ref=weights.at[d, 0], send_sem=wsend_sem.at[d], recv_sem=wrecv_sem.at[d],
            device_id=(2 * lax.rem(me_z + d, Z) + core, me_f), device_id_type=MESH)

    def forward_copy(d):
        return pltpu.make_async_remote_copy(
            src_ref=weights.at[d, 0], dst_ref=weights.at[d, 1], send_sem=fsend_sem.at[d], recv_sem=frecv_sem.at[d],
            device_id=(2 * me_z + 1 - core, me_f), device_id_type=MESH)

    def right_copy(k):
        return pltpu.make_async_remote_copy(
            src_ref=right, dst_ref=rights.at[k], send_sem=rsend_sem.at[k], recv_sem=rrecv_sem.at[k],
            device_id=(me_r, lax.rem(me_f + k, F)), device_id_type=MESH)

    def top_copy(k):
        return pltpu.make_async_remote_copy(
            src_ref=top, dst_ref=tops.at[k], send_sem=tsend_sem.at[k], recv_sem=trecv_sem.at[k],
            device_id=(lax.rem(me_r + k, R), me_f), device_id_type=MESH)

    def high_copy(k):
        return pltpu.make_async_remote_copy(
            src_ref=high, dst_ref=highs.at[k], send_sem=hsend_sem.at[k], recv_sem=hrecv_sem.at[k],
            device_id=(me_r, lax.rem(me_f + k, F)), device_id_type=MESH)

    def start(copy, k, c):
        copy(k).start()
        return c

    def wait_recv(copy, k, c):
        copy(k).wait_recv()
        return c

    def wait_send(copy, k, c):
        copy(k).wait_send()
        return c

    def distance(i):
        odd = lax.rem(i, 2)
        return odd * ((i + 1) // 2) + (1 - odd) * (Z - i // 2)

    forward_copy(0).start()
    bins_copy(0, 1).start()
    weights_copy(distance(1)).start()

    def send_round(i):
        @pl.when(i < Z - 1)
        def _():
            weights_copy(distance(i + 1)).start()

        bins_copy(distance(i), 0).start()
        bins_copy(distance(i), 1).start()

    def first_round(i, c):
        send_round(i)
        return c

    lax.fori_loop(1, FIRST + 1, first_round, 0)

    span = 2
    depth = span * LANES
    blocks_of_chunk = tiles // span
    zero = jnp.zeros((NODES, depth), BF16)
    high_rows = 2 * NODES * HI

    def over_lanes(ref, d, o, base, t, stride, rows):
        return jnp.concatenate(
            [jnp.broadcast_to(ref[d, o, pl.ds(base + (t * span + s) * stride, 1), :], (rows, LANES))
             for s in range(span)], axis=1)

    def push(chunk, t):
        d, o = chunk
        levels = as_bf16(sublane_index(LO, depth))
        steps = []
        for f in range(own):
            b = over_lanes(recv, d, o, f, t, own, 1).astype(jnp.float32)
            low = (b - jnp.floor(b * (1.0 / LO)) * LO).astype(BF16)
            steps.append(jnp.where(jnp.broadcast_to(low, (LO, depth)) <= levels, BF16(1), BF16(0)))
        pltpu.matmul_push_rhs(jnp.concatenate(steps, axis=0), (t // 2) % 2, t % 2, transpose=True)

    def stream(accs, chunk, t):
        d, o = chunk
        here = over_lanes(weights, d, o, 2 * tiles, t, 1, NODES) == as_bf16(sublane_index(NODES, depth))
        wg = jnp.where(here, over_lanes(weights, d, o, 0, t, 1, NODES), zero)
        wh = jnp.where(here, over_lanes(weights, d, o, tiles, t, 1, NODES), zero)
        sides = []
        for f in range(own):
            b = over_lanes(recv, d, o, f, t, own, 1).astype(jnp.float32)
            part = jnp.broadcast_to(jnp.floor(b * (1.0 / LO)).astype(BF16), (NODES, depth))
            for level in range(HI):
                at = part == BF16(level)
                sides += [jnp.where(at, wg, zero), jnp.where(at, wh, zero)]
        pltpu.matmul_acc_lhs(accs[t % 2], jnp.concatenate(sides, axis=0), (t // 2) % 2)

    def pass_on(d):
        weights_copy(d).wait_recv()
        forward_copy(d).start()

    def chunk_of(k):
        i = k // 2
        return jnp.where(i == 0, 0, distance(i)), lax.rem(k, 2)

    def await_chunk(k):
        d, o = chunk_of(k)
        bins_copy_from(d, o).wait_recv()

        @pl.when(o == 1)
        def _():
            forward_copy(d).wait_recv()

        return d, o

    def accumulate(*accs):
        push((0, 0), 0)
        push((0, 0), 1)

        def one_chunk(k, c):
            chunk = chunk_of(k)

            @pl.when((lax.rem(k, 2) == 1) & (k < R - 1))
            def _():
                pass_on(distance(k // 2 + 1))

            @pl.when((lax.rem(k, 2) == 0) & (k // 2 + FIRST + 1 < Z))
            def _():
                send_round(k // 2 + FIRST + 1)

            for t in range(blocks_of_chunk - 2):
                stream(accs, chunk, t)
                push(chunk, t + 2)
            following = await_chunk(k + 1)
            for t in range(blocks_of_chunk - 2, blocks_of_chunk):
                stream(accs, chunk, t)
                push(following, t + 2 - blocks_of_chunk)
            return c

        lax.fori_loop(0, R - 1, one_chunk, 0)
        chunk = chunk_of(R - 1)
        for t in range(blocks_of_chunk):
            stream(accs, chunk, t)
            if t + 2 < blocks_of_chunk:
                push(chunk, t + 2)
        total = pltpu.matmul_pop(accs[0]) + pltpu.matmul_pop(accs[1])
        for f in range(own):
            acc[f] = total[f * high_rows:(f + 1) * high_rows, f * LO:(f + 1) * LO]

    with jax.sharding.use_abstract_mesh(jax.sharding.get_abstract_mesh()):
        pl.run_scoped(
            accumulate,
            pltpu.ACC(0)((own * high_rows, own * LO), jnp.float32),
            pltpu.ACC(1)((own * high_rows, own * LO), jnp.float32))

    best = jnp.full((NODES, 1), -jnp.inf, jnp.float32)
    for f in range(own):
        blocks = []
        carry = jnp.zeros((2 * NODES, 1), jnp.float32)
        for level in range(HI):
            block = acc[f, level * 2 * NODES:(level + 1) * 2 * NODES, :] + carry
            carry = block[:, LO - 1:LO]
            blocks.append(block)
        left = jnp.concatenate(blocks, axis=1)
        left_grad, left_hess = left[:NODES], left[NODES:]
        total_grad, total_hess = carry[:NODES], carry[NODES:]
        right_grad = total_grad - left_grad
        gain = (left_grad * left_grad / (left_hess + 1.0)
                + right_grad * right_grad / (total_hess - left_hess + 1.0)
                - total_grad * total_grad / (total_hess + 1.0))
        gain_ref[f] = gain
        best = jnp.maximum(best, jnp.max(gain, axis=1, keepdims=True))

    index = sublane_index(NODES, LANES)
    diagonal = index == lax.broadcasted_iota(jnp.int32, (NODES, LANES), 1)
    top[...] = jnp.max(jnp.where(diagonal, best, -jnp.inf), axis=0, keepdims=True)
    tops[0] = top[...]
    lax.fori_loop(1, R, lambda k, c: start(top_copy, k, c), 0)

    first = me_f * feat_local
    split = jnp.zeros((NODES, LANES), jnp.int32)
    mine = jnp.zeros((NODES, LANES), jnp.int32)
    for n in range(NODES):
        column = sf_ref[n] - first
        held = jnp.where(column >= 0, 1, 0) * jnp.where(column < feat_local, 1, 0)
        picked[n:n + 1, :] = bins_v[pl.ds(jnp.clip(column, 0, feat_local - 1), 1), :]
        split = jnp.where(index == n, sb_ref[n], split)
        mine = jnp.where(index == n, held, mine)
    node_row = node_row_v[...]
    parts = []
    for t in range(tiles):
        lanes = slice(t * LANES, (t + 1) * LANES)
        goes = jnp.where(picked[:, lanes] > split, mine, 0)
        goes = jnp.where(jnp.broadcast_to(node_row[:, lanes], (NODES, LANES)) == index, goes, 0)
        parts.append(jnp.sum(goes.astype(jnp.float32), axis=0, keepdims=True))
    right[...] = jnp.concatenate(parts, axis=0).astype(BF16)
    lax.fori_loop(1, F, lambda k, c: start(right_copy, k, c), 0)

    lax.fori_loop(1, R, lambda k, c: wait_recv(top_copy, k, c), 0)
    high[...] = jnp.max(tops[...], axis=0)
    highs[0] = high[...]
    lax.fori_loop(1, F, lambda k, c: start(high_copy, k, c), 0)

    rights[0] = right[...]
    lax.fori_loop(1, F, lambda k, c: wait_recv(right_copy, k, c), 0)
    goes_right = jnp.zeros((tiles, LANES), jnp.float32)
    for k in range(F):
        goes_right = goes_right + rights[k].astype(jnp.float32)
    child_ref[...] = 2 * node_v[...] + goes_right.astype(jnp.int32)

    def sent(d, c):
        weights_copy(d).wait_send()
        bins_copy(d, 0).wait_send()
        bins_copy(d, 1).wait_send()
        forward_copy(d).wait_send()
        return c

    forward_copy(0).wait_send()
    bins_copy(0, 1).wait_send()
    lax.fori_loop(1, Z, sent, 0)
    lax.fori_loop(1, F, lambda k, c: wait_send(right_copy, k, c), 0)
    lax.fori_loop(1, R, lambda k, c: wait_send(top_copy, k, c), 0)
    lax.fori_loop(1, F, lambda k, c: wait_recv(high_copy, k, c), 0)
    best_ref[...] = jnp.max(highs[...], axis=0)
    lax.fori_loop(1, F, lambda k, c: wait_send(high_copy, k, c), 0)


def on_device(R, F, bin_index, gradient, hessian, node_id, split_feature, split_bin):
    feat_local, row_count = bin_index.shape
    own = feat_local // R
    tiles = row_count // LANES
    vmem = pl.BlockSpec(memory_space=pltpu.VMEM)
    smem = pl.BlockSpec(memory_space=pltpu.SMEM)
    hbm = pl.BlockSpec(memory_space=pltpu.HBM)
    dma = pltpu.SemaphoreType.DMA
    gain, best, child = pl.pallas_call(
        functools.partial(kernel, R, F, own),
        out_shape=(
            jax.ShapeDtypeStruct((own, NODES, BINS), jnp.float32),
            jax.ShapeDtypeStruct((1, LANES), jnp.float32),
            jax.ShapeDtypeStruct((tiles, LANES), jnp.int32),
        ),
        in_specs=[smem, smem, hbm, hbm, hbm, hbm, hbm],
        out_specs=(vmem, vmem, vmem),
        scratch_shapes=[
            pltpu.VMEM((feat_local, row_count), jnp.int32),
            pltpu.VMEM((NODES, row_count), jnp.int32),
            pltpu.VMEM((tiles, LANES), jnp.int32),
            pltpu.VMEM((1, row_count), jnp.int32),
            pltpu.VMEM((R, own * tiles, LANES), BF16),
            pltpu.VMEM((R // 2, 2, own * tiles, LANES), BF16),
            pltpu.VMEM((R // 2, 2, 3 * tiles, LANES), BF16),
            pltpu.VMEM((own, 2 * NODES * HI, LO), jnp.float32),
            pltpu.VMEM((tiles, LANES), BF16),
            pltpu.VMEM((F, tiles, LANES), BF16),
            pltpu.VMEM((1, LANES), jnp.float32),
            pltpu.VMEM((R, 1, LANES), jnp.float32),
            pltpu.VMEM((1, LANES), jnp.float32),
            pltpu.VMEM((F, 1, LANES), jnp.float32),
            dma((5,)),
            dma((R // 2, 2)), dma((R // 2, 2)),
            dma((R // 2,)), dma((R // 2,)),
            dma((R // 2,)), dma((R // 2,)),
            dma((F,)), dma((F,)),
            dma((R,)), dma((R,)),
            dma((F,)), dma((F,)),
        ],
        compiler_params=pltpu.CompilerParams(
            collective_id=0, has_side_effects=True, vmem_limit_bytes=60 << 20),
    )(
        split_feature, split_bin, bin_index,
        gradient.reshape(tiles, LANES), hessian.reshape(tiles, LANES),
        node_id.reshape(tiles, LANES), node_id.reshape(1, row_count),
    )
    return gain, best[0, :NODES], child.reshape(row_count)


def solution(mesh):
    return jax.shard_map(
        functools.partial(on_device, mesh.shape["rows"], mesh.shape["feats"]),
        mesh=mesh,
        in_specs=(P("feats", "rows"), P("rows"), P("rows"), P("rows"), P(), P()),
        out_specs=(P(("feats", "rows"), None, None), P(), P("rows")),
        check_vma=False,
    )
```

```python
import functools

import jax
import jax.numpy as jnp
from jax import lax
from jax.experimental import pallas as pl
from jax.experimental.pallas import tpu as pltpu
from jax.sharding import PartitionSpec as P

BINS = 256
LO = 64
HI = BINS // LO
NODES = 16
LANES = 128
BF16 = jnp.bfloat16
MESH = pl.DeviceIdType.MESH
FIRST = 3


def sublane_index(rows, lanes):
    return lax.broadcasted_iota(jnp.int32, (rows, lanes), 0)


def as_bf16(x):
    return x.astype(jnp.float32).astype(BF16)


def kernel(R, F, own, sf_ref, sb_ref, bins_ref, grad_ref, hess_ref, node_ref, node_row_ref,
           gain_ref, best_ref, child_ref,
           bins_v, picked, node_v, node_row_v, send, recv, weights, acc, right, rights, top, tops, high, highs,
           in_sem, send_sem, recv_sem, wsend_sem, wrecv_sem, fsend_sem, frecv_sem,
           rsend_sem, rrecv_sem, tsend_sem, trecv_sem, hsend_sem, hrecv_sem, column_in, all_in):
    feat_local, row_count = bins_v.shape
    tiles = row_count // LANES
    Z = R // 2
    me_r = lax.axis_index("rows")
    me_f = lax.axis_index("feats")
    me_z = me_r // 2
    core = lax.rem(me_r, 2)

    loads = [
        pltpu.make_async_copy(bins_ref, bins_v, in_sem.at[0]),
        pltpu.make_async_copy(grad_ref, weights.at[0, 0, 0:tiles, :], in_sem.at[1]),
        pltpu.make_async_copy(hess_ref, weights.at[0, 0, tiles:2 * tiles, :], in_sem.at[2]),
        pltpu.make_async_copy(node_ref, node_v, in_sem.at[3]),
        pltpu.make_async_copy(node_row_ref, node_row_v, in_sem.at[4]),
    ]
    for load in loads:
        load.start()

    Y = min(8, F)
    X = F // Y
    me_x, me_y = me_f // Y, lax.rem(me_f, Y)

    def feat_of(k):
        return lax.rem(me_x + k // Y, X) * Y + lax.rem(me_y + lax.rem(k, Y), Y)

    def hops(k):
        x, y = k // Y, k % Y
        return min(x, X - x) + min(y, Y - y)

    far_feats = sorted(range(1, F), key=lambda k: -hops(k))
    far_rows = sorted(range(1, R), key=lambda k: abs(k - R // 2))

    barrier = pltpu.get_barrier_semaphore()

    def greet_rows(k, c):
        pl.semaphore_signal(barrier, inc=1, device_id=(lax.rem(me_r + k, R), me_f), device_id_type=MESH)
        return c

    def over_feats(sem):
        def greet(k, c):
            pl.semaphore_signal(sem, inc=1, device_id=(me_r, feat_of(k)), device_id_type=MESH)
            return c

        lax.fori_loop(1, F, greet, 0)

    lax.fori_loop(R // 2, R, greet_rows, 0)
    lax.fori_loop(1, R // 2, greet_rows, 0)

    @pl.when(me_z == 0)
    def _():
        over_feats(barrier)

    for load in loads:
        load.wait()
    weights[0, 0, 2 * tiles:3 * tiles, :] = as_bf16(node_v[...])
    for j in range(R):
        block = bins_v[j * own:(j + 1) * own, :]
        send[j] = as_bf16(jnp.concatenate([block[:, t * LANES:(t + 1) * LANES] for t in range(tiles)], axis=0))
    recv[0, 0] = send[me_r]

    pl.semaphore_wait(barrier, jnp.where(me_z == 0, R + F - 2, R - 1))

    @pl.when(me_z == 0)
    def _():
        over_feats(column_in)

    def bins_copy(d, o):
        to = 2 * lax.rem(me_z + d, Z) + (core if o == 0 else 1 - core)
        return bins_copy_to(d, o, to)

    def bins_copy_from(d, o):
        return bins_copy_to(d, o, 2 * me_z + 1 - core)

    def bins_copy_to(d, o, to):
        return pltpu.make_async_remote_copy(
            src_ref=send.at[to], dst_ref=recv.at[d, o], send_sem=send_sem, recv_sem=recv_sem.at[d, o],
            device_id=(to, me_f), device_id_type=MESH)

    def weights_copy(d):
        return pltpu.make_async_remote_copy(
            src_ref=weights.at[0, 0], dst_ref=weights.at[d, 0], send_sem=wsend_sem, recv_sem=wrecv_sem.at[d],
            device_id=(2 * lax.rem(me_z + d, Z) + core, me_f), device_id_type=MESH)

    def forward_copy(d):
        return pltpu.make_async_remote_copy(
            src_ref=weights.at[d, 0], dst_ref=weights.at[d, 1], send_sem=fsend_sem, recv_sem=frecv_sem.at[d],
            device_id=(2 * me_z + 1 - core, me_f), device_id_type=MESH)

    def right_copy(k):
        return pltpu.make_async_remote_copy(
            src_ref=right, dst_ref=rights.at[k], send_sem=rsend_sem, recv_sem=rrecv_sem,
            device_id=(me_r, feat_of(k)), device_id_type=MESH)

    def top_copy(k):
        return pltpu.make_async_remote_copy(
            src_ref=top, dst_ref=tops.at[k], send_sem=tsend_sem, recv_sem=trecv_sem,
            device_id=(lax.rem(me_r + k, R), me_f), device_id_type=MESH)

    def high_copy(k):
        return pltpu.make_async_remote_copy(
            src_ref=high, dst_ref=highs.at[k], send_sem=hsend_sem, recv_sem=hrecv_sem,
            device_id=(me_r, feat_of(k)), device_id_type=MESH)

    def wait_bytes(ref, sem):
        pltpu.make_async_copy(ref, ref, sem).wait()

    def distance(i):
        odd = lax.rem(i, 2)
        return odd * ((i + 1) // 2) + (1 - odd) * (Z - i // 2)

    forward_copy(0).start()
    bins_copy(0, 1).start()
    weights_copy(distance(1)).start()

    def send_round(i):
        @pl.when(i < Z - 1)
        def _():
            weights_copy(distance(i + 1)).start()

        bins_copy(distance(i), 0).start()
        bins_copy(distance(i), 1).start()

    def first_round(i, c):
        send_round(i)
        return c

    lax.fori_loop(1, FIRST + 1, first_round, 0)

    span = 2
    depth = span * LANES
    blocks_of_chunk = tiles // span
    zero = jnp.zeros((NODES, depth), BF16)
    high_rows = 2 * NODES * HI

    def over_lanes(ref, d, o, base, t, stride, rows):
        return jnp.concatenate(
            [jnp.broadcast_to(ref[d, o, pl.ds(base + (t * span + s) * stride, 1), :], (rows, LANES))
             for s in range(span)], axis=1)

    def push(chunk, t):
        d, o = chunk
        levels = as_bf16(sublane_index(LO, depth))
        steps = []
        for f in range(own):
            b = over_lanes(recv, d, o, f, t, own, 1).astype(jnp.float32)
            low = (b - jnp.floor(b * (1.0 / LO)) * LO).astype(BF16)
            steps.append(jnp.where(jnp.broadcast_to(low, (LO, depth)) <= levels, BF16(1), BF16(0)))
        pltpu.matmul_push_rhs(jnp.concatenate(steps, axis=0), (t // 2) % 2, t % 2, transpose=True)

    def stream(accs, chunk, t):
        d, o = chunk
        here = over_lanes(weights, d, o, 2 * tiles, t, 1, NODES) == as_bf16(sublane_index(NODES, depth))
        wg = jnp.where(here, over_lanes(weights, d, o, 0, t, 1, NODES), zero)
        wh = jnp.where(here, over_lanes(weights, d, o, tiles, t, 1, NODES), zero)
        sides = []
        for f in range(own):
            b = over_lanes(recv, d, o, f, t, own, 1).astype(jnp.float32)
            part = jnp.broadcast_to(jnp.floor(b * (1.0 / LO)).astype(BF16), (NODES, depth))
            for level in range(HI):
                at = part == BF16(level)
                sides += [jnp.where(at, wg, zero), jnp.where(at, wh, zero)]
        pltpu.matmul_acc_lhs(accs[t % 2], jnp.concatenate(sides, axis=0), (t // 2) % 2)

    def pass_on(d):
        weights_copy(d).wait_recv()
        forward_copy(d).start()

    def chunk_of(k):
        i = k // 2
        return jnp.where(i == 0, 0, distance(i)), lax.rem(k, 2)

    def await_chunk(k):
        d, o = chunk_of(k)
        bins_copy_from(d, o).wait_recv()

        @pl.when(o == 1)
        def _():
            forward_copy(d).wait_recv()

        return d, o

    def accumulate(*accs):
        push((0, 0), 0)
        push((0, 0), 1)

        def one_chunk(k, c):
            chunk = chunk_of(k)

            @pl.when((lax.rem(k, 2) == 1) & (k < R - 1))
            def _():
                pass_on(distance(k // 2 + 1))

            @pl.when((lax.rem(k, 2) == 0) & (k // 2 + FIRST + 1 < Z))
            def _():
                send_round(k // 2 + FIRST + 1)

            @pl.when((me_z == 0) & (k == R // 2))
            def _():
                pl.semaphore_wait(column_in, F - 1)

                def tell(z, c):
                    pl.semaphore_signal(all_in, inc=1, device_id=(2 * z + core, me_f), device_id_type=MESH)
                    return c

                lax.fori_loop(1, Z, tell, 0)

            for t in range(blocks_of_chunk - 2):
                stream(accs, chunk, t)
                push(chunk, t + 2)
            following = await_chunk(k + 1)
            for t in range(blocks_of_chunk - 2, blocks_of_chunk):
                stream(accs, chunk, t)
                push(following, t + 2 - blocks_of_chunk)
            return c

        lax.fori_loop(0, R - 1, one_chunk, 0)
        chunk = chunk_of(R - 1)
        for t in range(blocks_of_chunk):
            stream(accs, chunk, t)
            if t + 2 < blocks_of_chunk:
                push(chunk, t + 2)
        total = pltpu.matmul_pop(accs[0]) + pltpu.matmul_pop(accs[1])
        for f in range(own):
            acc[f] = total[f * high_rows:(f + 1) * high_rows, f * LO:(f + 1) * LO]

    with jax.sharding.use_abstract_mesh(jax.sharding.get_abstract_mesh()):
        pl.run_scoped(
            accumulate,
            pltpu.ACC(0)((own * high_rows, own * LO), jnp.float32),
            pltpu.ACC(1)((own * high_rows, own * LO), jnp.float32))

    best = jnp.full((NODES, 1), -jnp.inf, jnp.float32)
    for f in range(own):
        blocks = []
        carry = jnp.zeros((2 * NODES, 1), jnp.float32)
        for level in range(HI):
            block = acc[f, level * 2 * NODES:(level + 1) * 2 * NODES, :] + carry
            carry = block[:, LO - 1:LO]
            blocks.append(block)
        left = jnp.concatenate(blocks, axis=1)
        left_grad, left_hess = left[:NODES], left[NODES:]
        total_grad, total_hess = carry[:NODES], carry[NODES:]
        right_grad = total_grad - left_grad
        gain = (left_grad * left_grad / (left_hess + 1.0)
                + right_grad * right_grad / (total_hess - left_hess + 1.0)
                - total_grad * total_grad / (total_hess + 1.0))
        gain_ref[f] = gain
        best = jnp.maximum(best, jnp.max(gain, axis=1, keepdims=True))

    index = sublane_index(NODES, LANES)
    diagonal = index == lax.broadcasted_iota(jnp.int32, (NODES, LANES), 1)
    top[...] = jnp.max(jnp.where(diagonal, best, -jnp.inf), axis=0, keepdims=True)
    tops[0] = top[...]
    for k in far_rows:
        top_copy(k).start()

    first = me_f * feat_local
    split = jnp.zeros((NODES, LANES), jnp.int32)
    mine = jnp.zeros((NODES, LANES), jnp.int32)
    for n in range(NODES):
        column = sf_ref[n] - first
        held = jnp.where(column >= 0, 1, 0) * jnp.where(column < feat_local, 1, 0)
        picked[n:n + 1, :] = bins_v[pl.ds(jnp.clip(column, 0, feat_local - 1), 1), :]
        split = jnp.where(index == n, sb_ref[n], split)
        mine = jnp.where(index == n, held, mine)
    node_row = node_row_v[...]
    parts = []
    for t in range(tiles):
        lanes = slice(t * LANES, (t + 1) * LANES)
        goes = jnp.where(picked[:, lanes] > split, mine, 0)
        goes = jnp.where(jnp.broadcast_to(node_row[:, lanes], (NODES, LANES)) == index, goes, 0)
        parts.append(jnp.sum(goes.astype(jnp.float32), axis=0, keepdims=True))
    right[...] = jnp.concatenate(parts, axis=0).astype(BF16)
    rights[0] = right[...]

    @pl.when(me_z > 0)
    def _():
        pl.semaphore_wait(all_in, 1)

    for k in far_feats:
        right_copy(k).start()

    wait_bytes(tops.at[pl.ds(1, R - 1)], trecv_sem)
    high[...] = jnp.max(tops[...], axis=0)
    highs[0] = high[...]
    for k in far_feats:
        high_copy(k).start()

    wait_bytes(rights.at[pl.ds(1, F - 1)], rrecv_sem)
    goes_right = jnp.zeros((tiles, LANES), jnp.float32)
    for k in range(F):
        goes_right = goes_right + rights[k].astype(jnp.float32)
    child_ref[...] = 2 * node_v[...] + goes_right.astype(jnp.int32)

    wait_bytes(send.at[pl.ds(0, R - 1)], send_sem)
    wait_bytes(weights.at[pl.ds(1, Z - 1), 0], wsend_sem)
    wait_bytes(weights.at[pl.ds(0, Z), 0], fsend_sem)
    wait_bytes(rights.at[pl.ds(1, F - 1)], rsend_sem)
    wait_bytes(tops.at[pl.ds(1, R - 1)], tsend_sem)
    wait_bytes(highs.at[pl.ds(1, F - 1)], hrecv_sem)
    best_ref[...] = jnp.max(highs[...], axis=0)
    wait_bytes(highs.at[pl.ds(1, F - 1)], hsend_sem)


def on_device(R, F, bin_index, gradient, hessian, node_id, split_feature, split_bin):
    feat_local, row_count = bin_index.shape
    own = feat_local // R
    tiles = row_count // LANES
    vmem = pl.BlockSpec(memory_space=pltpu.VMEM)
    smem = pl.BlockSpec(memory_space=pltpu.SMEM)
    hbm = pl.BlockSpec(memory_space=pltpu.HBM)
    dma = pltpu.SemaphoreType.DMA
    gain, best, child = pl.pallas_call(
        functools.partial(kernel, R, F, own),
        out_shape=(
            jax.ShapeDtypeStruct((own, NODES, BINS), jnp.float32),
            jax.ShapeDtypeStruct((1, LANES), jnp.float32),
            jax.ShapeDtypeStruct((tiles, LANES), jnp.int32),
        ),
        in_specs=[smem, smem, hbm, hbm, hbm, hbm, hbm],
        out_specs=(vmem, vmem, vmem),
        scratch_shapes=[
            pltpu.VMEM((feat_local, row_count), jnp.int32),
            pltpu.VMEM((NODES, row_count), jnp.int32),
            pltpu.VMEM((tiles, LANES), jnp.int32),
            pltpu.VMEM((1, row_count), jnp.int32),
            pltpu.VMEM((R, own * tiles, LANES), BF16),
            pltpu.VMEM((R // 2, 2, own * tiles, LANES), BF16),
            pltpu.VMEM((R // 2, 2, 3 * tiles, LANES), BF16),
            pltpu.VMEM((own, 2 * NODES * HI, LO), jnp.float32),
            pltpu.VMEM((tiles, LANES), BF16),
            pltpu.VMEM((F, tiles, LANES), BF16),
            pltpu.VMEM((1, LANES), jnp.float32),
            pltpu.VMEM((R, 1, LANES), jnp.float32),
            pltpu.VMEM((1, LANES), jnp.float32),
            pltpu.VMEM((F, 1, LANES), jnp.float32),
            dma((5,)),
            dma(()), dma((R // 2, 2)),
            dma(()), dma((R // 2,)),
            dma(()), dma((R // 2,)),
            dma(()), dma(()),
            dma(()), dma(()),
            dma(()), dma(()),
            pltpu.SemaphoreType.REGULAR,
            pltpu.SemaphoreType.REGULAR,
        ],
        compiler_params=pltpu.CompilerParams(
            collective_id=0, has_side_effects=True, vmem_limit_bytes=60 << 20),
    )(
        split_feature, split_bin, bin_index,
        gradient.reshape(tiles, LANES), hessian.reshape(tiles, LANES),
        node_id.reshape(tiles, LANES), node_id.reshape(1, row_count),
    )
    return gain, best[0, :NODES], child.reshape(row_count)


def solution(mesh):
    return jax.shard_map(
        functools.partial(on_device, mesh.shape["rows"], mesh.shape["feats"]),
        mesh=mesh,
        in_specs=(P("feats", "rows"), P("rows"), P("rows"), P("rows"), P(), P()),
        out_specs=(P(("feats", "rows"), None, None), P(), P("rows")),
        check_vma=False,
    )
```

```python
import functools

import jax
import jax.numpy as jnp
from jax import lax
from jax.experimental import pallas as pl
from jax.experimental.pallas import tpu as pltpu
from jax.sharding import PartitionSpec as P

BINS = 256
LO = 64
HI = BINS // LO
NODES = 16
LANES = 128
BF16 = jnp.bfloat16
MESH = pl.DeviceIdType.MESH
FIRST = 3


def sublane_index(rows, lanes):
    return lax.broadcasted_iota(jnp.int32, (rows, lanes), 0)


def as_bf16(x):
    return x.astype(jnp.float32).astype(BF16)


def kernel(R, F, own, sf_in, sb_in, bins_ref, grad_ref, hess_ref, node_ref, node_row_ref,
           gain_ref, best_ref, child_ref,
           sf_ref, sb_ref, bins_v, picked, node_v, node_row_v, send, recv, weights, acc, right, rights, top, tops, high, highs,
           in_sem, send_sem, recv_sem, wsend_sem, wrecv_sem, fsend_sem, frecv_sem,
           rsend_sem, rrecv_sem, tsend_sem, trecv_sem, hsend_sem, hrecv_sem, column_in, all_in):
    feat_local, row_count = bins_v.shape
    tiles = row_count // LANES
    Z = R // 2
    me_r = lax.axis_index("rows")
    me_f = lax.axis_index("feats")
    me_z = me_r // 2
    core = lax.rem(me_r, 2)

    loads = [
        pltpu.make_async_copy(bins_ref, bins_v, in_sem.at[0]),
        pltpu.make_async_copy(grad_ref, weights.at[0, 0, 0:tiles, :], in_sem.at[1]),
        pltpu.make_async_copy(hess_ref, weights.at[0, 0, tiles:2 * tiles, :], in_sem.at[2]),
        pltpu.make_async_copy(node_ref, node_v, in_sem.at[3]),
        pltpu.make_async_copy(node_row_ref, node_row_v, in_sem.at[4]),
        pltpu.make_async_copy(sf_in, sf_ref, in_sem.at[5]),
        pltpu.make_async_copy(sb_in, sb_ref, in_sem.at[6]),
    ]
    for load in loads:
        load.start()

    Y = min(8, F)
    X = F // Y
    me_x, me_y = me_f // Y, lax.rem(me_f, Y)

    def feat_of(k):
        return lax.rem(me_x + k // Y, X) * Y + lax.rem(me_y + lax.rem(k, Y), Y)

    def hops(k):
        x, y = k // Y, k % Y
        return min(x, X - x) + min(y, Y - y)

    far_feats = sorted(range(1, F), key=lambda k: -hops(k))
    far_rows = sorted(range(1, R), key=lambda k: abs(k - R // 2))

    barrier = pltpu.get_barrier_semaphore()

    def greet_rows(k, c):
        pl.semaphore_signal(barrier, inc=1, device_id=(lax.rem(me_r + k, R), me_f), device_id_type=MESH)
        return c

    def over_feats(sem):
        def greet(k, c):
            pl.semaphore_signal(sem, inc=1, device_id=(me_r, feat_of(k)), device_id_type=MESH)
            return c

        lax.fori_loop(1, F, greet, 0)

    lax.fori_loop(R // 2, R, greet_rows, 0)
    lax.fori_loop(1, R // 2, greet_rows, 0)

    @pl.when(me_z == 0)
    def _():
        over_feats(barrier)

    for load in loads:
        load.wait()
    weights[0, 0, 2 * tiles:3 * tiles, :] = as_bf16(node_v[...])
    for j in range(R):
        block = bins_v[j * own:(j + 1) * own, :]
        send[j] = as_bf16(jnp.concatenate([block[:, t * LANES:(t + 1) * LANES] for t in range(tiles)], axis=0))
    recv[0, 0] = send[me_r]

    pl.semaphore_wait(barrier, jnp.where(me_z == 0, R + F - 2, R - 1))

    @pl.when(me_z == 0)
    def _():
        over_feats(column_in)

    def bins_copy(d, o):
        to = 2 * lax.rem(me_z + d, Z) + (core if o == 0 else 1 - core)
        return bins_copy_to(d, o, to)

    def bins_copy_from(d, o):
        return bins_copy_to(d, o, 2 * me_z + 1 - core)

    def bins_copy_to(d, o, to):
        return pltpu.make_async_remote_copy(
            src_ref=send.at[to], dst_ref=recv.at[d, o], send_sem=send_sem, recv_sem=recv_sem.at[d, o],
            device_id=(to, me_f), device_id_type=MESH)

    def weights_copy(d):
        return pltpu.make_async_remote_copy(
            src_ref=weights.at[0, 0], dst_ref=weights.at[d, 0], send_sem=wsend_sem, recv_sem=wrecv_sem.at[d],
            device_id=(2 * lax.rem(me_z + d, Z) + core, me_f), device_id_type=MESH)

    def forward_copy(d):
        return pltpu.make_async_remote_copy(
            src_ref=weights.at[d, 0], dst_ref=weights.at[d, 1], send_sem=fsend_sem, recv_sem=frecv_sem.at[d],
            device_id=(2 * me_z + 1 - core, me_f), device_id_type=MESH)

    def right_copy(k):
        return pltpu.make_async_remote_copy(
            src_ref=right, dst_ref=rights.at[k], send_sem=rsend_sem, recv_sem=rrecv_sem,
            device_id=(me_r, feat_of(k)), device_id_type=MESH)

    def top_copy(k):
        return pltpu.make_async_remote_copy(
            src_ref=top, dst_ref=tops.at[k], send_sem=tsend_sem, recv_sem=trecv_sem,
            device_id=(lax.rem(me_r + k, R), me_f), device_id_type=MESH)

    def high_copy(k):
        return pltpu.make_async_remote_copy(
            src_ref=high, dst_ref=highs.at[k], send_sem=hsend_sem, recv_sem=hrecv_sem,
            device_id=(me_r, feat_of(k)), device_id_type=MESH)

    def wait_bytes(ref, sem):
        pltpu.make_async_copy(ref, ref, sem).wait()

    def distance(i):
        odd = lax.rem(i, 2)
        return odd * ((i + 1) // 2) + (1 - odd) * (Z - i // 2)

    forward_copy(0).start()
    bins_copy(0, 1).start()
    weights_copy(distance(1)).start()

    def send_round(i):
        @pl.when(i < Z - 1)
        def _():
            weights_copy(distance(i + 1)).start()

        bins_copy(distance(i), 0).start()
        bins_copy(distance(i), 1).start()

    def first_round(i, c):
        send_round(i)
        return c

    lax.fori_loop(1, FIRST + 1, first_round, 0)

    span = 2
    depth = span * LANES
    blocks_of_chunk = tiles // span
    zero = jnp.zeros((NODES, depth), BF16)
    high_rows = 2 * NODES * HI

    def over_lanes(ref, d, o, base, t, stride, rows):
        return jnp.concatenate(
            [jnp.broadcast_to(ref[d, o, pl.ds(base + (t * span + s) * stride, 1), :], (rows, LANES))
             for s in range(span)], axis=1)

    def push(chunk, t):
        d, o = chunk
        levels = as_bf16(sublane_index(LO, depth))
        steps = []
        for f in range(own):
            b = over_lanes(recv, d, o, f, t, own, 1).astype(jnp.float32)
            low = (b - jnp.floor(b * (1.0 / LO)) * LO).astype(BF16)
            steps.append(jnp.where(jnp.broadcast_to(low, (LO, depth)) <= levels, BF16(1), BF16(0)))
        pltpu.matmul_push_rhs(jnp.concatenate(steps, axis=0), (t // 2) % 2, t % 2, transpose=True)

    def stream(accs, chunk, t):
        d, o = chunk
        here = over_lanes(weights, d, o, 2 * tiles, t, 1, NODES) == as_bf16(sublane_index(NODES, depth))
        wg = jnp.where(here, over_lanes(weights, d, o, 0, t, 1, NODES), zero)
        wh = jnp.where(here, over_lanes(weights, d, o, tiles, t, 1, NODES), zero)
        sides = []
        for f in range(own):
            b = over_lanes(recv, d, o, f, t, own, 1).astype(jnp.float32)
            part = jnp.broadcast_to(jnp.floor(b * (1.0 / LO)).astype(BF16), (NODES, depth))
            for level in range(HI):
                at = part == BF16(level)
                sides += [jnp.where(at, wg, zero), jnp.where(at, wh, zero)]
        pltpu.matmul_acc_lhs(accs[t % 2], jnp.concatenate(sides, axis=0), (t // 2) % 2)

    def pass_on(d):
        weights_copy(d).wait_recv()
        forward_copy(d).start()

    def chunk_of(k):
        i = k // 2
        return jnp.where(i == 0, 0, distance(i)), lax.rem(k, 2)

    def await_chunk(k):
        d, o = chunk_of(k)
        bins_copy_from(d, o).wait_recv()

        @pl.when(o == 1)
        def _():
            forward_copy(d).wait_recv()

        return d, o

    def accumulate(*accs):
        push((0, 0), 0)
        push((0, 0), 1)

        def one_chunk(k, c):
            chunk = chunk_of(k)

            @pl.when((lax.rem(k, 2) == 1) & (k < R - 1))
            def _():
                pass_on(distance(k // 2 + 1))

            @pl.when((lax.rem(k, 2) == 0) & (k // 2 + FIRST + 1 < Z))
            def _():
                send_round(k // 2 + FIRST + 1)

            @pl.when((me_z == 0) & (k == R // 2))
            def _():
                pl.semaphore_wait(column_in, F - 1)

                def tell(z, c):
                    pl.semaphore_signal(all_in, inc=1, device_id=(2 * z + core, me_f), device_id_type=MESH)
                    return c

                lax.fori_loop(1, Z, tell, 0)

            for t in range(blocks_of_chunk - 2):
                stream(accs, chunk, t)
                push(chunk, t + 2)
            following = await_chunk(k + 1)
            for t in range(blocks_of_chunk - 2, blocks_of_chunk):
                stream(accs, chunk, t)
                push(following, t + 2 - blocks_of_chunk)
            return c

        lax.fori_loop(0, R - 1, one_chunk, 0)
        chunk = chunk_of(R - 1)
        for t in range(blocks_of_chunk):
            stream(accs, chunk, t)
            if t + 2 < blocks_of_chunk:
                push(chunk, t + 2)
        total = pltpu.matmul_pop(accs[0]) + pltpu.matmul_pop(accs[1])
        for f in range(own):
            acc[f] = total[f * high_rows:(f + 1) * high_rows, f * LO:(f + 1) * LO]

    with jax.sharding.use_abstract_mesh(jax.sharding.get_abstract_mesh()):
        pl.run_scoped(
            accumulate,
            pltpu.ACC(0)((own * high_rows, own * LO), jnp.float32),
            pltpu.ACC(1)((own * high_rows, own * LO), jnp.float32))

    best = jnp.full((NODES, 1), -jnp.inf, jnp.float32)
    for f in range(own):
        blocks = []
        carry = jnp.zeros((2 * NODES, 1), jnp.float32)
        for level in range(HI):
            block = acc[f, level * 2 * NODES:(level + 1) * 2 * NODES, :] + carry
            carry = block[:, LO - 1:LO]
            blocks.append(block)
        left = jnp.concatenate(blocks, axis=1)
        left_grad, left_hess = left[:NODES], left[NODES:]
        total_grad, total_hess = carry[:NODES], carry[NODES:]
        right_grad = total_grad - left_grad
        gain = (left_grad * left_grad / (left_hess + 1.0)
                + right_grad * right_grad / (total_hess - left_hess + 1.0)
                - total_grad * total_grad / (total_hess + 1.0))
        gain_ref[f] = gain
        best = jnp.maximum(best, jnp.max(gain, axis=1, keepdims=True))

    index = sublane_index(NODES, LANES)
    diagonal = index == lax.broadcasted_iota(jnp.int32, (NODES, LANES), 1)
    top[...] = jnp.max(jnp.where(diagonal, best, -jnp.inf), axis=0, keepdims=True)
    tops[0] = top[...]
    for k in far_rows:
        top_copy(k).start()

    first = me_f * feat_local
    split = jnp.zeros((NODES, LANES), jnp.int32)
    mine = jnp.zeros((NODES, LANES), jnp.int32)
    for n in range(NODES):
        column = sf_ref[n] - first
        held = jnp.where(column >= 0, 1, 0) * jnp.where(column < feat_local, 1, 0)
        picked[n:n + 1, :] = bins_v[pl.ds(jnp.clip(column, 0, feat_local - 1), 1), :]
        split = jnp.where(index == n, sb_ref[n], split)
        mine = jnp.where(index == n, held, mine)
    node_row = node_row_v[...]
    parts = []
    for t in range(tiles):
        lanes = slice(t * LANES, (t + 1) * LANES)
        goes = jnp.where(picked[:, lanes] > split, mine, 0)
        goes = jnp.where(jnp.broadcast_to(node_row[:, lanes], (NODES, LANES)) == index, goes, 0)
        parts.append(jnp.sum(goes.astype(jnp.float32), axis=0, keepdims=True))
    right[...] = jnp.concatenate(parts, axis=0).astype(BF16)
    rights[0] = right[...]

    @pl.when(me_z > 0)
    def _():
        pl.semaphore_wait(all_in, 1)

    for k in far_feats:
        right_copy(k).start()

    wait_bytes(tops.at[pl.ds(1, R - 1)], trecv_sem)
    high[...] = jnp.max(tops[...], axis=0)
    highs[0] = high[...]
    for k in far_feats:
        high_copy(k).start()

    wait_bytes(rights.at[pl.ds(1, F - 1)], rrecv_sem)
    goes_right = jnp.zeros((tiles, LANES), jnp.float32)
    for k in range(F):
        goes_right = goes_right + rights[k].astype(jnp.float32)
    child_ref[...] = 2 * node_v[...] + goes_right.astype(jnp.int32)

    wait_bytes(send.at[pl.ds(0, R - 1)], send_sem)
    wait_bytes(weights.at[pl.ds(1, Z - 1), 0], wsend_sem)
    wait_bytes(weights.at[pl.ds(0, Z), 0], fsend_sem)
    wait_bytes(rights.at[pl.ds(1, F - 1)], rsend_sem)
    wait_bytes(tops.at[pl.ds(1, R - 1)], tsend_sem)
    wait_bytes(highs.at[pl.ds(1, F - 1)], hrecv_sem)
    best_ref[...] = jnp.max(highs[...], axis=0)
    wait_bytes(highs.at[pl.ds(1, F - 1)], hsend_sem)


def finish(gain_in, best_in, child_in, gain_ref, best_ref, child_ref, sem):
    moves = [
        pltpu.make_async_copy(gain_in, gain_ref, sem.at[0]),
        pltpu.make_async_copy(child_in, child_ref, sem.at[1]),
    ]
    for move in moves:
        move.start()
    best_ref[...] = best_in[0, 0:NODES]
    for move in moves:
        move.wait()


def on_device(R, F, bin_index, gradient, hessian, node_id, split_feature, split_bin):
    feat_local, row_count = bin_index.shape
    own = feat_local // R
    tiles = row_count // LANES
    vmem = pl.BlockSpec(memory_space=pltpu.VMEM)
    hbm = pl.BlockSpec(memory_space=pltpu.HBM)
    dma = pltpu.SemaphoreType.DMA
    gain, best, child = pl.pallas_call(
        functools.partial(kernel, R, F, own),
        out_shape=(
            jax.ShapeDtypeStruct((own, NODES, BINS), jnp.float32),
            jax.ShapeDtypeStruct((1, LANES), jnp.float32),
            jax.ShapeDtypeStruct((tiles, LANES), jnp.int32),
        ),
        in_specs=[hbm] * 7,
        out_specs=(vmem, vmem, vmem),
        scratch_shapes=[
            pltpu.SMEM((NODES,), jnp.int32),
            pltpu.SMEM((NODES,), jnp.int32),
            pltpu.VMEM((feat_local, row_count), jnp.int32),
            pltpu.VMEM((NODES, row_count), jnp.int32),
            pltpu.VMEM((tiles, LANES), jnp.int32),
            pltpu.VMEM((1, row_count), jnp.int32),
            pltpu.VMEM((R, own * tiles, LANES), BF16),
            pltpu.VMEM((R // 2, 2, own * tiles, LANES), BF16),
            pltpu.VMEM((R // 2, 2, 3 * tiles, LANES), BF16),
            pltpu.VMEM((own, 2 * NODES * HI, LO), jnp.float32),
            pltpu.VMEM((tiles, LANES), BF16),
            pltpu.VMEM((F, tiles, LANES), BF16),
            pltpu.VMEM((1, LANES), jnp.float32),
            pltpu.VMEM((R, 1, LANES), jnp.float32),
            pltpu.VMEM((1, LANES), jnp.float32),
            pltpu.VMEM((F, 1, LANES), jnp.float32),
            dma((7,)),
            dma(()), dma((R // 2, 2)),
            dma(()), dma((R // 2,)),
            dma(()), dma((R // 2,)),
            dma(()), dma(()),
            dma(()), dma(()),
            dma(()), dma(()),
            pltpu.SemaphoreType.REGULAR,
            pltpu.SemaphoreType.REGULAR,
        ],
        compiler_params=pltpu.CompilerParams(
            collective_id=0, has_side_effects=True, vmem_limit_bytes=32 << 20),
    )(
        *(pltpu.with_memory_space_constraint(x, pltpu.HBM) for x in (
            split_feature, split_bin, bin_index,
            gradient.reshape(tiles, LANES), hessian.reshape(tiles, LANES),
            node_id.reshape(tiles, LANES), node_id.reshape(1, row_count)))
    )
    gain, best, child = pl.pallas_call(
        finish,
        out_shape=(
            jax.ShapeDtypeStruct(gain.shape, gain.dtype),
            jax.ShapeDtypeStruct((NODES,), best.dtype),
            jax.ShapeDtypeStruct(child.shape, child.dtype),
        ),
        in_specs=[vmem, vmem, vmem],
        out_specs=(hbm, vmem, hbm),
        scratch_shapes=[dma((2,))],
        compiler_params=pltpu.CompilerParams(vmem_limit_bytes=32 << 20),
    )(gain, best, child)
    return gain, best, child.reshape(row_count)


def solution(mesh):
    return jax.shard_map(
        functools.partial(on_device, mesh.shape["rows"], mesh.shape["feats"]),
        mesh=mesh,
        in_specs=(P("feats", "rows"), P("rows"), P("rows"), P("rows"), P(), P()),
        out_specs=(P(("feats", "rows"), None, None), P(), P("rows")),
        check_vma=False,
    )
```

```python
import functools

import jax
import jax.numpy as jnp
from jax import lax
from jax.experimental import pallas as pl
from jax.experimental.pallas import tpu as pltpu
from jax.sharding import PartitionSpec as P

BINS = 256
LO = 64
HI = BINS // LO
NODES = 16
LANES = 128
BF16 = jnp.bfloat16
MESH = pl.DeviceIdType.MESH
FIRST = 4


def sublane_index(rows, lanes):
    return lax.broadcasted_iota(jnp.int32, (rows, lanes), 0)


def as_bf16(x):
    return x.astype(jnp.float32).astype(BF16)


def kernel(R, F, own, sf_in, sb_in, bins_ref, grad_ref, hess_ref, node_ref, node_row_ref,
           gain_ref, best_ref, child_ref,
           sf_ref, sb_ref, bins_v, picked, node_v, node_row_v, send, recv, weights, acc, right, rights, top, tops, high, highs,
           in_sem, send_sem, recv_sem, wsend_sem, wrecv_sem, fsend_sem, frecv_sem,
           rsend_sem, rrecv_sem, tsend_sem, trecv_sem, hsend_sem, hrecv_sem, ready, column_in, all_in):
    feat_local, row_count = bins_v.shape
    tiles = row_count // LANES
    Z = R // 2
    me_r = lax.axis_index("rows")
    me_f = lax.axis_index("feats")
    me_z = me_r // 2
    core = lax.rem(me_r, 2)

    loads = [
        pltpu.make_async_copy(bins_ref, bins_v, in_sem.at[0]),
        pltpu.make_async_copy(grad_ref, weights.at[0, 0, 0:tiles, :], in_sem.at[1]),
        pltpu.make_async_copy(hess_ref, weights.at[0, 0, tiles:2 * tiles, :], in_sem.at[2]),
        pltpu.make_async_copy(node_ref, node_v, in_sem.at[3]),
        pltpu.make_async_copy(node_row_ref, node_row_v, in_sem.at[4]),
        pltpu.make_async_copy(sf_in, sf_ref, in_sem.at[5]),
        pltpu.make_async_copy(sb_in, sb_ref, in_sem.at[6]),
    ]
    Y = min(8, F)
    X = F // Y
    me_x, me_y = me_f // Y, lax.rem(me_f, Y)

    def feat_of(k):
        return lax.rem(me_x + k // Y, X) * Y + lax.rem(me_y + lax.rem(k, Y), Y)

    def hops(k):
        x, y = k // Y, k % Y
        return min(x, X - x) + min(y, Y - y)

    far_feats = sorted(range(1, F), key=lambda k: -hops(k))
    far_rows = sorted(range(1, R), key=lambda k: abs(k - R // 2))

    barrier = pltpu.get_barrier_semaphore()

    def over_rows(sem, first, last):
        def greet(r, c):
            pl.semaphore_signal(sem, inc=1, device_id=(r, me_f), device_id_type=MESH)
            return c

        lax.fori_loop(first, last, greet, 0)

    def over_feats(sem):
        def greet(k, c):
            pl.semaphore_signal(sem, inc=1, device_id=(me_r, feat_of(k)), device_id_type=MESH)
            return c

        lax.fori_loop(1, F, greet, 0)

    pl.semaphore_signal(barrier, inc=1, device_id=(2 * me_z + 1 - core, me_f), device_id_type=MESH)
    over_rows(barrier, 2 * (me_z + 1), R)

    @pl.when(me_z == 0)
    def _():
        over_feats(barrier)

    for load in loads:
        load.start()
    pl.semaphore_wait(barrier, jnp.where(me_z == 0, F, 2 * me_z + 1))
    over_rows(ready.at[me_r], 0, 2 * me_z)

    for load in loads:
        load.wait()
    weights[0, 0, 2 * tiles:3 * tiles, :] = as_bf16(node_v[...])
    for j in range(R):
        block = bins_v[j * own:(j + 1) * own, :]
        send[j] = as_bf16(jnp.concatenate([block[:, t * LANES:(t + 1) * LANES] for t in range(tiles)], axis=0))
    recv[0, 0] = send[me_r]

    def bins_copy(d, o):
        to = 2 * lax.rem(me_z + d, Z) + (core if o == 0 else 1 - core)
        return bins_copy_to(d, o, to)

    def bins_copy_from(d, o):
        return bins_copy_to(d, o, 2 * me_z + 1 - core)

    def bins_copy_to(d, o, to):
        return pltpu.make_async_remote_copy(
            src_ref=send.at[to], dst_ref=recv.at[d, o], send_sem=send_sem, recv_sem=recv_sem.at[d, o],
            device_id=(to, me_f), device_id_type=MESH)

    def weights_copy(d):
        return pltpu.make_async_remote_copy(
            src_ref=weights.at[0, 0], dst_ref=weights.at[d, 0], send_sem=wsend_sem, recv_sem=wrecv_sem.at[d],
            device_id=(2 * lax.rem(me_z + d, Z) + core, me_f), device_id_type=MESH)

    def forward_copy(d):
        return pltpu.make_async_remote_copy(
            src_ref=weights.at[d, 0], dst_ref=weights.at[d, 1], send_sem=fsend_sem, recv_sem=frecv_sem.at[d],
            device_id=(2 * me_z + 1 - core, me_f), device_id_type=MESH)

    def right_copy(k):
        return pltpu.make_async_remote_copy(
            src_ref=right, dst_ref=rights.at[k], send_sem=rsend_sem, recv_sem=rrecv_sem,
            device_id=(me_r, feat_of(k)), device_id_type=MESH)

    def top_copy(k):
        return pltpu.make_async_remote_copy(
            src_ref=top, dst_ref=tops.at[k], send_sem=tsend_sem, recv_sem=trecv_sem,
            device_id=(lax.rem(me_r + k, R), me_f), device_id_type=MESH)

    def high_copy(k):
        return pltpu.make_async_remote_copy(
            src_ref=high, dst_ref=highs.at[k], send_sem=hsend_sem, recv_sem=hrecv_sem,
            device_id=(me_r, feat_of(k)), device_id_type=MESH)

    def wait_bytes(ref, sem):
        pltpu.make_async_copy(ref, ref, sem).wait()

    def distance(i):
        odd = lax.rem(i, 2)
        return odd * ((i + 1) // 2) + (1 - odd) * (Z - i // 2)

    forward_copy(0).start()
    bins_copy(0, 1).start()
    def send_weights(d):
        @pl.when(me_z + d < Z)
        def _():
            for o in range(2):
                pl.semaphore_wait(ready.at[2 * (me_z + d) + o], 1)

        weights_copy(d).start()

    def send_round(i):
        bins_copy(distance(i), 0).start()
        bins_copy(distance(i), 1).start()

        @pl.when(i < Z - 1)
        def _():
            send_weights(distance(i + 1))

    send_weights(distance(1))

    def first_round(i, c):
        send_round(i)
        return c

    lax.fori_loop(1, min(FIRST, Z - 1) + 1, first_round, 0)

    span = 2
    depth = span * LANES
    blocks_of_chunk = tiles // span
    zero = jnp.zeros((NODES, depth), BF16)
    high_rows = 2 * NODES * HI
    MET = max(2, Z - FIRST) + 1

    def over_lanes(ref, d, o, base, t, stride, rows):
        return jnp.concatenate(
            [jnp.broadcast_to(ref[d, o, pl.ds(base + (t * span + s) * stride, 1), :], (rows, LANES))
             for s in range(span)], axis=1)

    def push(chunk, t):
        d, o = chunk
        levels = as_bf16(sublane_index(LO, depth))
        steps = []
        for f in range(own):
            b = over_lanes(recv, d, o, f, t, own, 1).astype(jnp.float32)
            low = (b - jnp.floor(b * (1.0 / LO)) * LO).astype(BF16)
            steps.append(jnp.where(jnp.broadcast_to(low, (LO, depth)) <= levels, BF16(1), BF16(0)))
        pltpu.matmul_push_rhs(jnp.concatenate(steps, axis=0), (t // 2) % 2, t % 2, transpose=True)

    def stream(accs, chunk, t):
        d, o = chunk
        here = over_lanes(weights, d, o, 2 * tiles, t, 1, NODES) == as_bf16(sublane_index(NODES, depth))
        wg = jnp.where(here, over_lanes(weights, d, o, 0, t, 1, NODES), zero)
        wh = jnp.where(here, over_lanes(weights, d, o, tiles, t, 1, NODES), zero)
        sides = []
        for f in range(own):
            b = over_lanes(recv, d, o, f, t, own, 1).astype(jnp.float32)
            part = jnp.broadcast_to(jnp.floor(b * (1.0 / LO)).astype(BF16), (NODES, depth))
            for level in range(HI):
                at = part == BF16(level)
                sides += [jnp.where(at, wg, zero), jnp.where(at, wh, zero)]
        pltpu.matmul_acc_lhs(accs[t % 2], jnp.concatenate(sides, axis=0), (t // 2) % 2)

    def pass_on(d):
        weights_copy(d).wait_recv()
        forward_copy(d).start()

    def chunk_of(k):
        i = k // 2
        return jnp.where(i == 0, 0, distance(i)), lax.rem(k, 2)

    def await_chunk(k):
        d, o = chunk_of(k)
        bins_copy_from(d, o).wait_recv()

        @pl.when(o == 1)
        def _():
            forward_copy(d).wait_recv()

        return d, o

    def accumulate(*accs):
        push((0, 0), 0)
        push((0, 0), 1)

        def one_chunk(k, c):
            chunk = chunk_of(k)

            @pl.when((lax.rem(k, 2) == 1) & (k < R - 1))
            def _():
                pass_on(distance(k // 2 + 1))

            @pl.when((k >= 2) & (k - 1 + FIRST < Z))
            def _():
                send_round(k - 1 + FIRST)

            @pl.when((me_z == 0) & (k == MET))
            def _():
                over_feats(column_in)

            @pl.when((me_z == 0) & (k == R - 3))
            def _():
                pl.semaphore_wait(column_in, F - 1)

                def tell(z, c):
                    pl.semaphore_signal(all_in, inc=1, device_id=(2 * z + core, me_f), device_id_type=MESH)
                    return c

                lax.fori_loop(1, Z, tell, 0)

            for t in range(blocks_of_chunk - 2):
                stream(accs, chunk, t)
                push(chunk, t + 2)
            following = await_chunk(k + 1)
            for t in range(blocks_of_chunk - 2, blocks_of_chunk):
                stream(accs, chunk, t)
                push(following, t + 2 - blocks_of_chunk)
            return c

        lax.fori_loop(0, R - 1, one_chunk, 0)
        chunk = chunk_of(R - 1)
        for t in range(blocks_of_chunk):
            stream(accs, chunk, t)
            if t + 2 < blocks_of_chunk:
                push(chunk, t + 2)
        total = pltpu.matmul_pop(accs[0]) + pltpu.matmul_pop(accs[1])
        for f in range(own):
            acc[f] = total[f * high_rows:(f + 1) * high_rows, f * LO:(f + 1) * LO]

    with jax.sharding.use_abstract_mesh(jax.sharding.get_abstract_mesh()):
        pl.run_scoped(
            accumulate,
            pltpu.ACC(0)((own * high_rows, own * LO), jnp.float32),
            pltpu.ACC(1)((own * high_rows, own * LO), jnp.float32))

    best = jnp.full((NODES, 1), -jnp.inf, jnp.float32)
    for f in range(own):
        blocks = []
        carry = jnp.zeros((2 * NODES, 1), jnp.float32)
        for level in range(HI):
            block = acc[f, level * 2 * NODES:(level + 1) * 2 * NODES, :] + carry
            carry = block[:, LO - 1:LO]
            blocks.append(block)
        left = jnp.concatenate(blocks, axis=1)
        left_grad, left_hess = left[:NODES], left[NODES:]
        total_grad, total_hess = carry[:NODES], carry[NODES:]
        right_grad = total_grad - left_grad
        gain = (left_grad * left_grad / (left_hess + 1.0)
                + right_grad * right_grad / (total_hess - left_hess + 1.0)
                - total_grad * total_grad / (total_hess + 1.0))
        gain_ref[f] = gain
        best = jnp.maximum(best, jnp.max(gain, axis=1, keepdims=True))

    index = sublane_index(NODES, LANES)
    diagonal = index == lax.broadcasted_iota(jnp.int32, (NODES, LANES), 1)
    top[...] = jnp.max(jnp.where(diagonal, best, -jnp.inf), axis=0, keepdims=True)
    tops[0] = top[...]
    for k in far_rows:
        top_copy(k).start()

    first = me_f * feat_local
    split = jnp.zeros((NODES, LANES), jnp.int32)
    mine = jnp.zeros((NODES, LANES), jnp.int32)
    for n in range(NODES):
        column = sf_ref[n] - first
        held = jnp.where(column >= 0, 1, 0) * jnp.where(column < feat_local, 1, 0)
        picked[n:n + 1, :] = bins_v[pl.ds(jnp.clip(column, 0, feat_local - 1), 1), :]
        split = jnp.where(index == n, sb_ref[n], split)
        mine = jnp.where(index == n, held, mine)
    node_row = node_row_v[...]
    parts = []
    for t in range(tiles):
        lanes = slice(t * LANES, (t + 1) * LANES)
        goes = jnp.where(picked[:, lanes] > split, mine, 0)
        goes = jnp.where(jnp.broadcast_to(node_row[:, lanes], (NODES, LANES)) == index, goes, 0)
        parts.append(jnp.sum(goes.astype(jnp.float32), axis=0, keepdims=True))
    right[...] = jnp.concatenate(parts, axis=0).astype(BF16)
    rights[0] = right[...]

    @pl.when(me_z > 0)
    def _():
        pl.semaphore_wait(all_in, 1)

    for k in far_feats:
        right_copy(k).start()

    wait_bytes(tops.at[pl.ds(1, R - 1)], trecv_sem)
    high[...] = jnp.max(tops[...], axis=0)
    highs[0] = high[...]
    for k in far_feats:
        high_copy(k).start()

    wait_bytes(rights.at[pl.ds(1, F - 1)], rrecv_sem)
    goes_right = jnp.zeros((tiles, LANES), jnp.float32)
    for k in range(F):
        goes_right = goes_right + rights[k].astype(jnp.float32)
    child_ref[...] = 2 * node_v[...] + goes_right.astype(jnp.int32)

    wait_bytes(send.at[pl.ds(0, R - 1)], send_sem)
    wait_bytes(weights.at[pl.ds(1, Z - 1), 0], wsend_sem)
    wait_bytes(weights.at[pl.ds(0, Z), 0], fsend_sem)
    wait_bytes(rights.at[pl.ds(1, F - 1)], rsend_sem)
    wait_bytes(tops.at[pl.ds(1, R - 1)], tsend_sem)
    wait_bytes(highs.at[pl.ds(1, F - 1)], hrecv_sem)
    best_ref[...] = jnp.max(highs[...], axis=0)
    wait_bytes(highs.at[pl.ds(1, F - 1)], hsend_sem)


def finish(gain_in, best_in, child_in, gain_ref, best_ref, child_ref, best_v, sem):
    moves = [
        pltpu.make_async_copy(gain_in, gain_ref, sem.at[0]),
        pltpu.make_async_copy(child_in, child_ref, sem.at[1]),
        pltpu.make_async_copy(best_v, best_ref, sem.at[2]),
    ]
    moves[0].start()
    moves[1].start()
    best_v[...] = best_in[0, 0:NODES]
    moves[2].start()
    for move in moves:
        move.wait()


def on_device(R, F, bin_index, gradient, hessian, node_id, split_feature, split_bin):
    feat_local, row_count = bin_index.shape
    own = feat_local // R
    tiles = row_count // LANES
    vmem = pl.BlockSpec(memory_space=pltpu.VMEM)
    hbm = pl.BlockSpec(memory_space=pltpu.HBM)
    dma = pltpu.SemaphoreType.DMA
    gain, best, child = pl.pallas_call(
        functools.partial(kernel, R, F, own),
        out_shape=(
            jax.ShapeDtypeStruct((own, NODES, BINS), jnp.float32),
            jax.ShapeDtypeStruct((1, LANES), jnp.float32),
            jax.ShapeDtypeStruct((tiles, LANES), jnp.int32),
        ),
        in_specs=[hbm] * 7,
        out_specs=(vmem, vmem, vmem),
        scratch_shapes=[
            pltpu.SMEM((NODES,), jnp.int32),
            pltpu.SMEM((NODES,), jnp.int32),
            pltpu.VMEM((feat_local, row_count), jnp.int32),
            pltpu.VMEM((NODES, row_count), jnp.int32),
            pltpu.VMEM((tiles, LANES), jnp.int32),
            pltpu.VMEM((1, row_count), jnp.int32),
            pltpu.VMEM((R, own * tiles, LANES), BF16),
            pltpu.VMEM((R // 2, 2, own * tiles, LANES), BF16),
            pltpu.VMEM((R // 2, 2, 3 * tiles, LANES), BF16),
            pltpu.VMEM((own, 2 * NODES * HI, LO), jnp.float32),
            pltpu.VMEM((tiles, LANES), BF16),
            pltpu.VMEM((F, tiles, LANES), BF16),
            pltpu.VMEM((1, LANES), jnp.float32),
            pltpu.VMEM((R, 1, LANES), jnp.float32),
            pltpu.VMEM((1, LANES), jnp.float32),
            pltpu.VMEM((F, 1, LANES), jnp.float32),
            dma((7,)),
            dma(()), dma((R // 2, 2)),
            dma(()), dma((R // 2,)),
            dma(()), dma((R // 2,)),
            dma(()), dma(()),
            dma(()), dma(()),
            dma(()), dma(()),
            pltpu.SemaphoreType.REGULAR((R,)),
            pltpu.SemaphoreType.REGULAR,
            pltpu.SemaphoreType.REGULAR,
        ],
        compiler_params=pltpu.CompilerParams(
            collective_id=0, has_side_effects=True, vmem_limit_bytes=32 << 20),
    )(
        *(pltpu.with_memory_space_constraint(x, pltpu.HBM) for x in (
            split_feature, split_bin, bin_index,
            gradient.reshape(tiles, LANES), hessian.reshape(tiles, LANES),
            node_id.reshape(tiles, LANES), node_id.reshape(1, row_count)))
    )
    gain, best, child = pl.pallas_call(
        finish,
        out_shape=(
            jax.ShapeDtypeStruct(gain.shape, gain.dtype),
            jax.ShapeDtypeStruct((NODES,), best.dtype),
            jax.ShapeDtypeStruct(child.shape, child.dtype),
        ),
        in_specs=[vmem, vmem, vmem],
        out_specs=(hbm, hbm, hbm),
        scratch_shapes=[pltpu.VMEM((NODES,), best.dtype), dma((3,))],
        compiler_params=pltpu.CompilerParams(vmem_limit_bytes=32 << 20),
    )(gain, best, child)
    return gain, best, child.reshape(row_count)


def solution(mesh):
    return jax.shard_map(
        functools.partial(on_device, mesh.shape["rows"], mesh.shape["feats"]),
        mesh=mesh,
        in_specs=(P("feats", "rows"), P("rows"), P("rows"), P("rows"), P(), P()),
        out_specs=(P(("feats", "rows"), None, None), P(), P("rows")),
        check_vma=False,
    )
```

```python
import functools

import jax
import jax.numpy as jnp
from jax import lax
from jax.experimental import pallas as pl
from jax.experimental.pallas import tpu as pltpu
from jax.sharding import PartitionSpec as P

BINS = 256
LO = 64
HI = BINS // LO
NODES = 16
LANES = 128
BF16 = jnp.bfloat16
MESH = pl.DeviceIdType.MESH
FIRST = 4


def sublane_index(rows, lanes):
    return lax.broadcasted_iota(jnp.int32, (rows, lanes), 0)


def as_bf16(x):
    return x.astype(jnp.float32).astype(BF16)


def kernel(R, F, own, sf_in, sb_in, bins_ref, grad_ref, hess_ref, node_ref, node_row_ref,
           gain_ref, best_ref, child_ref,
           sf_ref, sb_ref, bins_v, picked, node_v, node_row_v, send, recv, weights, acc, right, rights, top, tops, high, highs,
           in_sem, send_sem, recv_sem, wsend_sem, wrecv_sem, fsend_sem, frecv_sem,
           rsend_sem, rrecv_sem, tsend_sem, trecv_sem, hsend_sem, hrecv_sem, ready, column_in, all_in):
    feat_local, row_count = bins_v.shape
    tiles = row_count // LANES
    Z = R // 2
    me_r = lax.axis_index("rows")
    me_f = lax.axis_index("feats")
    me_z = me_r // 2
    core = lax.rem(me_r, 2)

    loads = [
        pltpu.make_async_copy(bins_ref, bins_v, in_sem.at[0]),
        pltpu.make_async_copy(grad_ref, weights.at[0, 0, 0:tiles, :], in_sem.at[1]),
        pltpu.make_async_copy(hess_ref, weights.at[0, 0, tiles:2 * tiles, :], in_sem.at[2]),
        pltpu.make_async_copy(node_ref, node_v, in_sem.at[3]),
        pltpu.make_async_copy(node_row_ref, node_row_v, in_sem.at[4]),
        pltpu.make_async_copy(sf_in, sf_ref, in_sem.at[5]),
        pltpu.make_async_copy(sb_in, sb_ref, in_sem.at[6]),
    ]
    Y = min(8, F)
    X = F // Y
    me_x, me_y = me_f // Y, lax.rem(me_f, Y)

    def feat_of(k):
        return lax.rem(me_x + k // Y, X) * Y + lax.rem(me_y + lax.rem(k, Y), Y)

    def hops(k):
        x, y = k // Y, k % Y
        return min(x, X - x) + min(y, Y - y)

    far_feats = sorted(range(1, F), key=lambda k: -hops(k))
    far_rows = sorted(range(1, R), key=lambda k: abs(k - R // 2))

    barrier = pltpu.get_barrier_semaphore()

    def over_rows(sem, first, last):
        def greet(r, c):
            pl.semaphore_signal(sem, inc=1, device_id=(r, me_f), device_id_type=MESH)
            return c

        lax.fori_loop(first, last, greet, 0)

    def over_feats(sem):
        def greet(k, c):
            pl.semaphore_signal(sem, inc=1, device_id=(me_r, feat_of(k)), device_id_type=MESH)
            return c

        lax.fori_loop(1, F, greet, 0)

    pl.semaphore_signal(barrier, inc=1, device_id=(2 * me_z + 1 - core, me_f), device_id_type=MESH)
    over_rows(barrier, 2 * (me_z + 1), R)

    @pl.when(me_z == 0)
    def _():
        over_feats(barrier)

    for load in loads:
        load.start()
    pl.semaphore_wait(barrier, jnp.where(me_z == 0, F, 2 * me_z + 1))
    over_rows(ready.at[me_r], 0, 2 * me_z)

    for load in loads:
        load.wait()
    weights[0, 0, 2 * tiles:3 * tiles, :] = as_bf16(node_v[...])
    for j in range(R):
        block = bins_v[j * own:(j + 1) * own, :]
        send[j] = as_bf16(jnp.concatenate([block[:, t * LANES:(t + 1) * LANES] for t in range(tiles)], axis=0))
    recv[0, 0] = send[me_r]

    def bins_copy(d, o):
        to = 2 * lax.rem(me_z + d, Z) + (core if o == 0 else 1 - core)
        return bins_copy_to(d, o, to)

    def bins_copy_from(d, o):
        return bins_copy_to(d, o, 2 * me_z + 1 - core)

    def bins_copy_to(d, o, to):
        return pltpu.make_async_remote_copy(
            src_ref=send.at[to], dst_ref=recv.at[d, o], send_sem=send_sem, recv_sem=recv_sem.at[d, o],
            device_id=(to, me_f), device_id_type=MESH)

    def weights_copy(d):
        return pltpu.make_async_remote_copy(
            src_ref=weights.at[0, 0], dst_ref=weights.at[d, 0], send_sem=wsend_sem, recv_sem=wrecv_sem.at[d],
            device_id=(2 * lax.rem(me_z + d, Z) + core, me_f), device_id_type=MESH)

    def forward_copy(d):
        return pltpu.make_async_remote_copy(
            src_ref=weights.at[d, 0], dst_ref=weights.at[d, 1], send_sem=fsend_sem, recv_sem=frecv_sem.at[d],
            device_id=(2 * me_z + 1 - core, me_f), device_id_type=MESH)

    def right_copy(k):
        return pltpu.make_async_remote_copy(
            src_ref=right, dst_ref=rights.at[k], send_sem=rsend_sem, recv_sem=rrecv_sem,
            device_id=(me_r, feat_of(k)), device_id_type=MESH)

    def top_copy(k):
        return pltpu.make_async_remote_copy(
            src_ref=top, dst_ref=tops.at[k], send_sem=tsend_sem, recv_sem=trecv_sem,
            device_id=(lax.rem(me_r + k, R), me_f), device_id_type=MESH)

    def high_copy(k):
        return pltpu.make_async_remote_copy(
            src_ref=high, dst_ref=highs.at[k], send_sem=hsend_sem, recv_sem=hrecv_sem,
            device_id=(me_r, feat_of(k)), device_id_type=MESH)

    def wait_bytes(ref, sem):
        pltpu.make_async_copy(ref, ref, sem).wait()

    def distance(i):
        odd = lax.rem(i, 2)
        return odd * ((i + 1) // 2) + (1 - odd) * (Z - i // 2)

    forward_copy(0).start()
    bins_copy(0, 1).start()
    def send_weights(d):
        @pl.when(me_z + d < Z)
        def _():
            for o in range(2):
                pl.semaphore_wait(ready.at[2 * (me_z + d) + o], 1)

        weights_copy(d).start()

    def send_round(i):
        bins_copy(distance(i), 0).start()
        bins_copy(distance(i), 1).start()

        @pl.when(i < Z - 1)
        def _():
            send_weights(distance(i + 1))

    send_weights(distance(1))

    def first_round(i, c):
        send_round(i)
        return c

    lax.fori_loop(1, min(FIRST, Z - 1) + 1, first_round, 0)

    span = 2
    depth = span * LANES
    blocks_of_chunk = tiles // span
    zero = jnp.zeros((NODES, depth), BF16)
    high_rows = 2 * NODES * HI
    MET = max(3, Z - FIRST + 1) + 1

    def over_lanes(ref, d, o, base, t, stride, rows):
        return jnp.concatenate(
            [jnp.broadcast_to(ref[d, o, pl.ds(base + (t * span + s) * stride, 1), :], (rows, LANES))
             for s in range(span)], axis=1)

    def push(chunk, t):
        d, o = chunk
        levels = as_bf16(sublane_index(LO, depth))
        steps = []
        for f in range(own):
            b = over_lanes(recv, d, o, f, t, own, 1).astype(jnp.float32)
            low = (b - jnp.floor(b * (1.0 / LO)) * LO).astype(BF16)
            steps.append(jnp.where(jnp.broadcast_to(low, (LO, depth)) <= levels, BF16(1), BF16(0)))
        pltpu.matmul_push_rhs(jnp.concatenate(steps, axis=0), (t // 2) % 2, t % 2, transpose=True)

    def stream(accs, chunk, t):
        d, o = chunk
        here = over_lanes(weights, d, o, 2 * tiles, t, 1, NODES) == as_bf16(sublane_index(NODES, depth))
        wg = jnp.where(here, over_lanes(weights, d, o, 0, t, 1, NODES), zero)
        wh = jnp.where(here, over_lanes(weights, d, o, tiles, t, 1, NODES), zero)
        sides = []
        for f in range(own):
            b = over_lanes(recv, d, o, f, t, own, 1).astype(jnp.float32)
            part = jnp.broadcast_to(jnp.floor(b * (1.0 / LO)).astype(BF16), (NODES, depth))
            for level in range(HI):
                at = part == BF16(level)
                sides += [jnp.where(at, wg, zero), jnp.where(at, wh, zero)]
        pltpu.matmul_acc_lhs(accs[t % 2], jnp.concatenate(sides, axis=0), (t // 2) % 2)

    def pass_on(d):
        weights_copy(d).wait_recv()
        forward_copy(d).start()

    def chunk_of(k):
        i = k // 2
        return jnp.where(i == 0, 0, distance(i)), lax.rem(k, 2)

    def await_chunk(k):
        d, o = chunk_of(k)
        bins_copy_from(d, o).wait_recv()

        @pl.when(o == 1)
        def _():
            forward_copy(d).wait_recv()

        return d, o

    def accumulate(*accs):
        push((0, 0), 0)
        push((0, 0), 1)

        def one_chunk(k, c):
            chunk = chunk_of(k)

            @pl.when((lax.rem(k, 2) == 1) & (k < R - 1))
            def _():
                pass_on(distance(k // 2 + 1))

            @pl.when((k >= 3) & (k - 2 + FIRST < Z))
            def _():
                send_round(k - 2 + FIRST)

            @pl.when((me_z == 0) & (k == MET))
            def _():
                over_feats(column_in)

            @pl.when((me_z == 0) & (k == R - 3))
            def _():
                pl.semaphore_wait(column_in, F - 1)

                def tell(z, c):
                    pl.semaphore_signal(all_in, inc=1, device_id=(2 * z + core, me_f), device_id_type=MESH)
                    return c

                lax.fori_loop(1, Z, tell, 0)

            for t in range(blocks_of_chunk - 2):
                stream(accs, chunk, t)
                push(chunk, t + 2)
            following = await_chunk(k + 1)
            for t in range(blocks_of_chunk - 2, blocks_of_chunk):
                stream(accs, chunk, t)
                push(following, t + 2 - blocks_of_chunk)
            return c

        lax.fori_loop(0, R - 1, one_chunk, 0)
        chunk = chunk_of(R - 1)
        for t in range(blocks_of_chunk):
            stream(accs, chunk, t)
            if t + 2 < blocks_of_chunk:
                push(chunk, t + 2)
        total = pltpu.matmul_pop(accs[0]) + pltpu.matmul_pop(accs[1])
        for f in range(own):
            acc[f] = total[f * high_rows:(f + 1) * high_rows, f * LO:(f + 1) * LO]

    with jax.sharding.use_abstract_mesh(jax.sharding.get_abstract_mesh()):
        pl.run_scoped(
            accumulate,
            pltpu.ACC(0)((own * high_rows, own * LO), jnp.float32),
            pltpu.ACC(1)((own * high_rows, own * LO), jnp.float32))

    highest = jnp.full((NODES, BINS), -jnp.inf, jnp.float32)
    for f in range(own):
        parts = [acc[f, level * 2 * NODES:(level + 1) * 2 * NODES, :] for level in range(HI)]
        carry = jnp.zeros((2 * NODES, 1), jnp.float32)
        blocks = []
        for part in parts:
            blocks.append(part + carry)
            carry = part[:, LO - 1:LO] + carry
        left = jnp.concatenate(blocks, axis=1)
        left_grad, left_hess = left[:NODES], left[NODES:]
        total_grad, total_hess = carry[:NODES], carry[NODES:]
        right_grad = total_grad - left_grad
        gain = (left_grad * left_grad / (left_hess + 1.0)
                + right_grad * right_grad / (total_hess - left_hess + 1.0)
                - total_grad * total_grad / (total_hess + 1.0))
        gain_ref[f] = gain
        highest = jnp.maximum(highest, gain)
    best = jnp.max(highest, axis=1, keepdims=True)

    index = sublane_index(NODES, LANES)
    diagonal = index == lax.broadcasted_iota(jnp.int32, (NODES, LANES), 1)
    top[...] = jnp.max(jnp.where(diagonal, best, -jnp.inf), axis=0, keepdims=True)
    tops[0] = top[...]
    for k in far_rows:
        top_copy(k).start()

    first = me_f * feat_local
    split = jnp.zeros((NODES, LANES), jnp.int32)
    mine = jnp.zeros((NODES, LANES), jnp.int32)
    for n in range(NODES):
        column = sf_ref[n] - first
        held = jnp.where(column >= 0, 1, 0) * jnp.where(column < feat_local, 1, 0)
        picked[n:n + 1, :] = bins_v[pl.ds(jnp.clip(column, 0, feat_local - 1), 1), :]
        split = jnp.where(index == n, sb_ref[n], split)
        mine = jnp.where(index == n, held, mine)
    node_row = node_row_v[...]
    parts = []
    for t in range(tiles):
        lanes = slice(t * LANES, (t + 1) * LANES)
        goes = jnp.where(picked[:, lanes] > split, mine, 0)
        goes = jnp.where(jnp.broadcast_to(node_row[:, lanes], (NODES, LANES)) == index, goes, 0)
        parts.append(jnp.sum(goes.astype(jnp.float32), axis=0, keepdims=True))
    right[...] = jnp.concatenate(parts, axis=0).astype(BF16)
    rights[0] = right[...]

    @pl.when(me_z > 0)
    def _():
        pl.semaphore_wait(all_in, 1)

    for k in far_feats:
        right_copy(k).start()

    wait_bytes(tops.at[pl.ds(1, R - 1)], trecv_sem)
    high[...] = jnp.max(tops[...], axis=0)
    highs[0] = high[...]
    for k in far_feats:
        high_copy(k).start()

    wait_bytes(rights.at[pl.ds(1, F - 1)], rrecv_sem)
    goes_right = jnp.zeros((tiles, LANES), jnp.float32)
    for k in range(F):
        goes_right = goes_right + rights[k].astype(jnp.float32)
    child_ref[...] = 2 * node_v[...] + goes_right.astype(jnp.int32)

    wait_bytes(send.at[pl.ds(0, R - 1)], send_sem)
    wait_bytes(weights.at[pl.ds(1, Z - 1), 0], wsend_sem)
    wait_bytes(weights.at[pl.ds(0, Z), 0], fsend_sem)
    wait_bytes(rights.at[pl.ds(1, F - 1)], rsend_sem)
    wait_bytes(tops.at[pl.ds(1, R - 1)], tsend_sem)
    wait_bytes(highs.at[pl.ds(1, F - 1)], hrecv_sem)
    best_ref[...] = jnp.max(highs[...], axis=0)
    wait_bytes(highs.at[pl.ds(1, F - 1)], hsend_sem)


def finish(gain_in, best_in, child_in, gain_ref, best_ref, child_ref, best_v, sem):
    moves = [
        pltpu.make_async_copy(gain_in, gain_ref, sem.at[0]),
        pltpu.make_async_copy(child_in, child_ref, sem.at[1]),
        pltpu.make_async_copy(best_v, best_ref, sem.at[2]),
    ]
    moves[0].start()
    moves[1].start()
    best_v[...] = best_in[0, 0:NODES]
    moves[2].start()
    for move in moves:
        move.wait()


def on_device(R, F, bin_index, gradient, hessian, node_id, split_feature, split_bin):
    feat_local, row_count = bin_index.shape
    own = feat_local // R
    tiles = row_count // LANES
    vmem = pl.BlockSpec(memory_space=pltpu.VMEM)
    hbm = pl.BlockSpec(memory_space=pltpu.HBM)
    dma = pltpu.SemaphoreType.DMA
    gain, best, child = pl.pallas_call(
        functools.partial(kernel, R, F, own),
        out_shape=(
            jax.ShapeDtypeStruct((own, NODES, BINS), jnp.float32),
            jax.ShapeDtypeStruct((1, LANES), jnp.float32),
            jax.ShapeDtypeStruct((tiles, LANES), jnp.int32),
        ),
        in_specs=[hbm] * 7,
        out_specs=(vmem, vmem, vmem),
        scratch_shapes=[
            pltpu.SMEM((NODES,), jnp.int32),
            pltpu.SMEM((NODES,), jnp.int32),
            pltpu.VMEM((feat_local, row_count), jnp.int32),
            pltpu.VMEM((NODES, row_count), jnp.int32),
            pltpu.VMEM((tiles, LANES), jnp.int32),
            pltpu.VMEM((1, row_count), jnp.int32),
            pltpu.VMEM((R, own * tiles, LANES), BF16),
            pltpu.VMEM((R // 2, 2, own * tiles, LANES), BF16),
            pltpu.VMEM((R // 2, 2, 3 * tiles, LANES), BF16),
            pltpu.VMEM((own, 2 * NODES * HI, LO), jnp.float32),
            pltpu.VMEM((tiles, LANES), BF16),
            pltpu.VMEM((F, tiles, LANES), BF16),
            pltpu.VMEM((1, LANES), jnp.float32),
            pltpu.VMEM((R, 1, LANES), jnp.float32),
            pltpu.VMEM((1, LANES), jnp.float32),
            pltpu.VMEM((F, 1, LANES), jnp.float32),
            dma((7,)),
            dma(()), dma((R // 2, 2)),
            dma(()), dma((R // 2,)),
            dma(()), dma((R // 2,)),
            dma(()), dma(()),
            dma(()), dma(()),
            dma(()), dma(()),
            pltpu.SemaphoreType.REGULAR((R,)),
            pltpu.SemaphoreType.REGULAR,
            pltpu.SemaphoreType.REGULAR,
        ],
        compiler_params=pltpu.CompilerParams(
            collective_id=0, has_side_effects=True, vmem_limit_bytes=32 << 20),
    )(
        *(pltpu.with_memory_space_constraint(x, pltpu.HBM) for x in (
            split_feature, split_bin, bin_index,
            gradient.reshape(tiles, LANES), hessian.reshape(tiles, LANES),
            node_id.reshape(tiles, LANES), node_id.reshape(1, row_count)))
    )
    gain, best, child = pl.pallas_call(
        finish,
        out_shape=(
            jax.ShapeDtypeStruct(gain.shape, gain.dtype),
            jax.ShapeDtypeStruct((NODES,), best.dtype),
            jax.ShapeDtypeStruct(child.shape, child.dtype),
        ),
        in_specs=[vmem, vmem, vmem],
        out_specs=(hbm, hbm, hbm),
        scratch_shapes=[pltpu.VMEM((NODES,), best.dtype), dma((3,))],
        compiler_params=pltpu.CompilerParams(vmem_limit_bytes=32 << 20),
    )(gain, best, child)
    return gain, best, child.reshape(row_count)


def solution(mesh):
    return jax.shard_map(
        functools.partial(on_device, mesh.shape["rows"], mesh.shape["feats"]),
        mesh=mesh,
        in_specs=(P("feats", "rows"), P("rows"), P("rows"), P("rows"), P(), P()),
        out_specs=(P(("feats", "rows"), None, None), P(), P("rows")),
        check_vma=False,
    )
```

```python
import functools

import jax
import jax.numpy as jnp
from jax import lax
from jax.experimental import pallas as pl
from jax.experimental.pallas import tpu as pltpu
from jax.sharding import PartitionSpec as P

BINS = 256
LO = 64
HI = BINS // LO
NODES = 16
LANES = 128
BF16 = jnp.bfloat16
MESH = pl.DeviceIdType.MESH
FIRST = 4


def sublane_index(rows, lanes):
    return lax.broadcasted_iota(jnp.int32, (rows, lanes), 0)


def as_bf16(x):
    return x.astype(jnp.float32).astype(BF16)


def kernel(R, F, own, sf_in, sb_in, bins_ref, grad_ref, hess_ref, node_ref, node_row_ref,
           gain_ref, best_ref, child_ref,
           sf_ref, sb_ref, bins_v, picked, node_v, node_row_v, send, recv, weights, acc, right, rights, top, tops, high, highs,
           in_sem, send_sem, recv_sem, wsend_sem, wrecv_sem, fsend_sem, frecv_sem,
           rsend_sem, rrecv_sem, tsend_sem, trecv_sem, hsend_sem, hrecv_sem, ready, column_in, all_in):
    feat_local, row_count = bins_v.shape
    tiles = row_count // LANES
    Z = R // 2
    me_r = lax.axis_index("rows")
    me_f = lax.axis_index("feats")
    me_z = me_r // 2
    core = lax.rem(me_r, 2)

    loads = [
        pltpu.make_async_copy(bins_ref, bins_v, in_sem.at[0]),
        pltpu.make_async_copy(grad_ref, weights.at[0, 0, 0:tiles, :], in_sem.at[1]),
        pltpu.make_async_copy(hess_ref, weights.at[0, 0, tiles:2 * tiles, :], in_sem.at[2]),
        pltpu.make_async_copy(node_ref, node_v, in_sem.at[3]),
        pltpu.make_async_copy(node_row_ref, node_row_v, in_sem.at[4]),
        pltpu.make_async_copy(sf_in, sf_ref, in_sem.at[5]),
        pltpu.make_async_copy(sb_in, sb_ref, in_sem.at[6]),
    ]
    Y = min(8, F)
    X = F // Y
    me_x, me_y = me_f // Y, lax.rem(me_f, Y)

    def feat_of(k):
        return lax.rem(me_x + k // Y, X) * Y + lax.rem(me_y + lax.rem(k, Y), Y)

    def hops(k):
        x, y = k // Y, k % Y
        return min(x, X - x) + min(y, Y - y)

    far_feats = sorted(range(1, F), key=lambda k: -hops(k))
    far_rows = sorted(range(1, R), key=lambda k: abs(k - R // 2))

    barrier = pltpu.get_barrier_semaphore()

    def over_rows(sem, first, last):
        def greet(r, c):
            pl.semaphore_signal(sem, inc=1, device_id=(r, me_f), device_id_type=MESH)
            return c

        lax.fori_loop(first, last, greet, 0)

    def over_feats(sem):
        def greet(k, c):
            pl.semaphore_signal(sem, inc=1, device_id=(me_r, feat_of(k)), device_id_type=MESH)
            return c

        lax.fori_loop(1, F, greet, 0)

    pl.semaphore_signal(barrier, inc=1, device_id=(2 * me_z + 1 - core, me_f), device_id_type=MESH)
    over_rows(barrier, 2 * (me_z + 1), R)

    @pl.when(me_z == 0)
    def _():
        over_feats(barrier)

    for load in loads:
        load.start()
    pl.semaphore_wait(barrier, jnp.where(me_z == 0, F, 2 * me_z + 1))
    farthest = 2 * jnp.maximum(me_z - Z // 2, 0)
    over_rows(ready.at[me_r], farthest, 2 * me_z)
    over_rows(ready.at[me_r], 0, farthest)

    for load in loads:
        load.wait()
    weights[0, 0, 2 * tiles:3 * tiles, :] = as_bf16(node_v[...])
    for j in range(R):
        block = bins_v[j * own:(j + 1) * own, :]
        send[j] = as_bf16(jnp.concatenate([block[:, t * LANES:(t + 1) * LANES] for t in range(tiles)], axis=0))
    recv[0, 0] = send[me_r]

    def bins_copy(d, o):
        to = 2 * lax.rem(me_z + d, Z) + (core if o == 0 else 1 - core)
        return bins_copy_to(d, o, to)

    def bins_copy_from(d, o):
        return bins_copy_to(d, o, 2 * me_z + 1 - core)

    def bins_copy_to(d, o, to):
        return pltpu.make_async_remote_copy(
            src_ref=send.at[to], dst_ref=recv.at[d, o], send_sem=send_sem, recv_sem=recv_sem.at[d, o],
            device_id=(to, me_f), device_id_type=MESH)

    def weights_copy(d):
        return pltpu.make_async_remote_copy(
            src_ref=weights.at[0, 0], dst_ref=weights.at[d, 0], send_sem=wsend_sem, recv_sem=wrecv_sem.at[d],
            device_id=(2 * lax.rem(me_z + d, Z) + core, me_f), device_id_type=MESH)

    def forward_copy(d):
        return pltpu.make_async_remote_copy(
            src_ref=weights.at[d, 0], dst_ref=weights.at[d, 1], send_sem=fsend_sem, recv_sem=frecv_sem.at[d],
            device_id=(2 * me_z + 1 - core, me_f), device_id_type=MESH)

    def right_copy(k):
        return pltpu.make_async_remote_copy(
            src_ref=right, dst_ref=rights.at[k], send_sem=rsend_sem, recv_sem=rrecv_sem,
            device_id=(me_r, feat_of(k)), device_id_type=MESH)

    def top_copy(k):
        return pltpu.make_async_remote_copy(
            src_ref=top, dst_ref=tops.at[k], send_sem=tsend_sem, recv_sem=trecv_sem,
            device_id=(lax.rem(me_r + k, R), me_f), device_id_type=MESH)

    def high_copy(k):
        return pltpu.make_async_remote_copy(
            src_ref=high, dst_ref=highs.at[k], send_sem=hsend_sem, recv_sem=hrecv_sem,
            device_id=(me_r, feat_of(k)), device_id_type=MESH)

    def wait_bytes(ref, sem):
        pltpu.make_async_copy(ref, ref, sem).wait()

    def distance(i):
        odd = lax.rem(i, 2)
        return odd * ((i + 1) // 2) + (1 - odd) * (Z - i // 2)

    forward_copy(0).start()
    bins_copy(0, 1).start()
    def send_weights(d):
        @pl.when(me_z + d < Z)
        def _():
            for o in range(2):
                pl.semaphore_wait(ready.at[2 * (me_z + d) + o], 1)

        weights_copy(d).start()

    def send_round(i):
        bins_copy(distance(i), 0).start()
        bins_copy(distance(i), 1).start()

        @pl.when(i < Z - 1)
        def _():
            send_weights(distance(i + 1))

    send_weights(distance(1))

    def first_round(i, c):
        send_round(i)
        return c

    lax.fori_loop(1, min(FIRST, Z - 1) + 1, first_round, 0)

    span = 2
    depth = span * LANES
    blocks_of_chunk = tiles // span
    zero = jnp.zeros((NODES, depth), BF16)
    high_rows = 2 * NODES * HI
    MET = max(3, Z - FIRST + 1) + 1

    def over_lanes(ref, d, o, base, t, stride, rows):
        return jnp.concatenate(
            [jnp.broadcast_to(ref[d, o, pl.ds(base + (t * span + s) * stride, 1), :], (rows, LANES))
             for s in range(span)], axis=1)

    def push(chunk, t):
        d, o = chunk
        levels = as_bf16(sublane_index(LO, depth))
        steps = []
        for f in range(own):
            b = over_lanes(recv, d, o, f, t, own, 1).astype(jnp.float32)
            low = (b - jnp.floor(b * (1.0 / LO)) * LO).astype(BF16)
            steps.append(jnp.where(jnp.broadcast_to(low, (LO, depth)) <= levels, BF16(1), BF16(0)))
        pltpu.matmul_push_rhs(jnp.concatenate(steps, axis=0), (t // 2) % 2, t % 2, transpose=True)

    def stream(accs, chunk, t):
        d, o = chunk
        here = over_lanes(weights, d, o, 2 * tiles, t, 1, NODES) == as_bf16(sublane_index(NODES, depth))
        wg = jnp.where(here, over_lanes(weights, d, o, 0, t, 1, NODES), zero)
        wh = jnp.where(here, over_lanes(weights, d, o, tiles, t, 1, NODES), zero)
        sides = []
        for f in range(own):
            b = over_lanes(recv, d, o, f, t, own, 1).astype(jnp.float32)
            part = jnp.broadcast_to(jnp.floor(b * (1.0 / LO)).astype(BF16), (NODES, depth))
            for level in range(HI):
                at = part == BF16(level)
                sides += [jnp.where(at, wg, zero), jnp.where(at, wh, zero)]
        pltpu.matmul_acc_lhs(accs[t % 2], jnp.concatenate(sides, axis=0), (t // 2) % 2)

    def pass_on(d):
        weights_copy(d).wait_recv()
        forward_copy(d).start()

    def chunk_of(k):
        i = k // 2
        return jnp.where(i == 0, 0, distance(i)), lax.rem(k, 2)

    def await_chunk(k):
        d, o = chunk_of(k)
        bins_copy_from(d, o).wait_recv()

        @pl.when(o == 1)
        def _():
            forward_copy(d).wait_recv()

        return d, o

    def accumulate(*accs):
        push((0, 0), 0)
        push((0, 0), 1)

        def one_chunk(k, c):
            chunk = chunk_of(k)

            @pl.when((lax.rem(k, 2) == 1) & (k < R - 1))
            def _():
                pass_on(distance(k // 2 + 1))

            @pl.when((k >= 3) & (k - 2 + FIRST < Z))
            def _():
                send_round(k - 2 + FIRST)

            @pl.when((me_z == 0) & (k == MET))
            def _():
                over_feats(column_in)

            @pl.when((me_z == 0) & (k == R - 3))
            def _():
                pl.semaphore_wait(column_in, F - 1)

                def tell(z, c):
                    pl.semaphore_signal(all_in, inc=1, device_id=(2 * z + core, me_f), device_id_type=MESH)
                    return c

                lax.fori_loop(1, Z, tell, 0)

            for t in range(blocks_of_chunk - 2):
                stream(accs, chunk, t)
                push(chunk, t + 2)
            following = await_chunk(k + 1)
            for t in range(blocks_of_chunk - 2, blocks_of_chunk):
                stream(accs, chunk, t)
                push(following, t + 2 - blocks_of_chunk)
            return c

        lax.fori_loop(0, R - 1, one_chunk, 0)
        chunk = chunk_of(R - 1)
        for t in range(blocks_of_chunk):
            stream(accs, chunk, t)
            if t + 2 < blocks_of_chunk:
                push(chunk, t + 2)
        total = pltpu.matmul_pop(accs[0]) + pltpu.matmul_pop(accs[1])
        for f in range(own):
            acc[f] = total[f * high_rows:(f + 1) * high_rows, f * LO:(f + 1) * LO]

    with jax.sharding.use_abstract_mesh(jax.sharding.get_abstract_mesh()):
        pl.run_scoped(
            accumulate,
            pltpu.ACC(0)((own * high_rows, own * LO), jnp.float32),
            pltpu.ACC(1)((own * high_rows, own * LO), jnp.float32))

    highest = jnp.full((NODES, BINS), -jnp.inf, jnp.float32)
    for f in range(own):
        parts = [acc[f, level * 2 * NODES:(level + 1) * 2 * NODES, :] for level in range(HI)]
        carry = jnp.zeros((2 * NODES, 1), jnp.float32)
        blocks = []
        for part in parts:
            blocks.append(part + carry)
            carry = part[:, LO - 1:LO] + carry
        left = jnp.concatenate(blocks, axis=1)
        left_grad, left_hess = left[:NODES], left[NODES:]
        total_grad, total_hess = carry[:NODES], carry[NODES:]
        right_grad = total_grad - left_grad
        gain = (left_grad * left_grad / (left_hess + 1.0)
                + right_grad * right_grad / (total_hess - left_hess + 1.0)
                - total_grad * total_grad / (total_hess + 1.0))
        gain_ref[f] = gain
        highest = jnp.maximum(highest, gain)
    best = jnp.max(highest, axis=1, keepdims=True)

    index = sublane_index(NODES, LANES)
    diagonal = index == lax.broadcasted_iota(jnp.int32, (NODES, LANES), 1)
    top[...] = jnp.max(jnp.where(diagonal, best, -jnp.inf), axis=0, keepdims=True)
    tops[0] = top[...]
    for k in far_rows:
        top_copy(k).start()

    first = me_f * feat_local
    split = jnp.zeros((NODES, LANES), jnp.int32)
    mine = jnp.zeros((NODES, LANES), jnp.int32)
    for n in range(NODES):
        column = sf_ref[n] - first
        held = jnp.where(column >= 0, 1, 0) * jnp.where(column < feat_local, 1, 0)
        picked[n:n + 1, :] = bins_v[pl.ds(jnp.clip(column, 0, feat_local - 1), 1), :]
        split = jnp.where(index == n, sb_ref[n], split)
        mine = jnp.where(index == n, held, mine)
    node_row = node_row_v[...]
    parts = []
    for t in range(tiles):
        lanes = slice(t * LANES, (t + 1) * LANES)
        goes = jnp.where(picked[:, lanes] > split, mine, 0)
        goes = jnp.where(jnp.broadcast_to(node_row[:, lanes], (NODES, LANES)) == index, goes, 0)
        parts.append(jnp.sum(goes.astype(jnp.float32), axis=0, keepdims=True))
    right[...] = jnp.concatenate(parts, axis=0).astype(BF16)
    rights[0] = right[...]

    @pl.when(me_z > 0)
    def _():
        pl.semaphore_wait(all_in, 1)

    for k in far_feats:
        right_copy(k).start()

    wait_bytes(tops.at[pl.ds(1, R - 1)], trecv_sem)
    high[...] = jnp.max(tops[...], axis=0)
    highs[0] = high[...]
    for k in far_feats:
        high_copy(k).start()

    wait_bytes(rights.at[pl.ds(1, F - 1)], rrecv_sem)
    goes_right = jnp.zeros((tiles, LANES), jnp.float32)
    for k in range(F):
        goes_right = goes_right + rights[k].astype(jnp.float32)
    child_ref[...] = 2 * node_v[...] + goes_right.astype(jnp.int32)

    wait_bytes(send.at[pl.ds(0, R - 1)], send_sem)
    wait_bytes(weights.at[pl.ds(1, Z - 1), 0], wsend_sem)
    wait_bytes(weights.at[pl.ds(0, Z), 0], fsend_sem)
    wait_bytes(rights.at[pl.ds(1, F - 1)], rsend_sem)
    wait_bytes(tops.at[pl.ds(1, R - 1)], tsend_sem)
    wait_bytes(highs.at[pl.ds(1, F - 1)], hrecv_sem)
    best_ref[...] = jnp.max(highs[...], axis=0)
    wait_bytes(highs.at[pl.ds(1, F - 1)], hsend_sem)


def finish(gain_in, best_in, child_in, gain_ref, best_ref, child_ref, best_v, sem):
    moves = [
        pltpu.make_async_copy(gain_in, gain_ref, sem.at[0]),
        pltpu.make_async_copy(child_in, child_ref, sem.at[1]),
        pltpu.make_async_copy(best_v, best_ref, sem.at[2]),
    ]
    moves[0].start()
    moves[1].start()
    best_v[...] = best_in[0, 0:NODES]
    moves[2].start()
    for move in moves:
        move.wait()


def on_device(R, F, bin_index, gradient, hessian, node_id, split_feature, split_bin):
    feat_local, row_count = bin_index.shape
    own = feat_local // R
    tiles = row_count // LANES
    vmem = pl.BlockSpec(memory_space=pltpu.VMEM)
    hbm = pl.BlockSpec(memory_space=pltpu.HBM)
    dma = pltpu.SemaphoreType.DMA
    gain, best, child = pl.pallas_call(
        functools.partial(kernel, R, F, own),
        out_shape=(
            jax.ShapeDtypeStruct((own, NODES, BINS), jnp.float32),
            jax.ShapeDtypeStruct((1, LANES), jnp.float32),
            jax.ShapeDtypeStruct((tiles, LANES), jnp.int32),
        ),
        in_specs=[hbm] * 7,
        out_specs=(vmem, vmem, vmem),
        scratch_shapes=[
            pltpu.SMEM((NODES,), jnp.int32),
            pltpu.SMEM((NODES,), jnp.int32),
            pltpu.VMEM((feat_local, row_count), jnp.int32),
            pltpu.VMEM((NODES, row_count), jnp.int32),
            pltpu.VMEM((tiles, LANES), jnp.int32),
            pltpu.VMEM((1, row_count), jnp.int32),
            pltpu.VMEM((R, own * tiles, LANES), BF16),
            pltpu.VMEM((R // 2, 2, own * tiles, LANES), BF16),
            pltpu.VMEM((R // 2, 2, 3 * tiles, LANES), BF16),
            pltpu.VMEM((own, 2 * NODES * HI, LO), jnp.float32),
            pltpu.VMEM((tiles, LANES), BF16),
            pltpu.VMEM((F, tiles, LANES), BF16),
            pltpu.VMEM((1, LANES), jnp.float32),
            pltpu.VMEM((R, 1, LANES), jnp.float32),
            pltpu.VMEM((1, LANES), jnp.float32),
            pltpu.VMEM((F, 1, LANES), jnp.float32),
            dma((7,)),
            dma(()), dma((R // 2, 2)),
            dma(()), dma((R // 2,)),
            dma(()), dma((R // 2,)),
            dma(()), dma(()),
            dma(()), dma(()),
            dma(()), dma(()),
            pltpu.SemaphoreType.REGULAR((R,)),
            pltpu.SemaphoreType.REGULAR,
            pltpu.SemaphoreType.REGULAR,
        ],
        compiler_params=pltpu.CompilerParams(
            collective_id=0, has_side_effects=True, vmem_limit_bytes=32 << 20),
    )(
        *(pltpu.with_memory_space_constraint(x, pltpu.HBM) for x in (
            split_feature, split_bin, bin_index,
            gradient.reshape(tiles, LANES), hessian.reshape(tiles, LANES),
            node_id.reshape(tiles, LANES), node_id.reshape(1, row_count)))
    )
    gain, best, child = pl.pallas_call(
        finish,
        out_shape=(
            jax.ShapeDtypeStruct(gain.shape, gain.dtype),
            jax.ShapeDtypeStruct((NODES,), best.dtype),
            jax.ShapeDtypeStruct(child.shape, child.dtype),
        ),
        in_specs=[vmem, vmem, vmem],
        out_specs=(hbm, hbm, hbm),
        scratch_shapes=[pltpu.VMEM((NODES,), best.dtype), dma((3,))],
        compiler_params=pltpu.CompilerParams(vmem_limit_bytes=32 << 20),
    )(gain, best, child)
    return gain, best, child.reshape(row_count)


def solution(mesh):
    return jax.shard_map(
        functools.partial(on_device, mesh.shape["rows"], mesh.shape["feats"]),
        mesh=mesh,
        in_specs=(P("feats", "rows"), P("rows"), P("rows"), P("rows"), P(), P()),
        out_specs=(P(("feats", "rows"), None, None), P(), P("rows")),
        check_vma=False,
    )
```
